32 devices in a mesh: dp: 8 (over z, y), section: 2 (over core), tensor: 2 (over x).
Axes of the slice: x: 2, y: 2, z: 4, core: 2. Of those that a mesh axis runs over, the one named last changes fastest.
Arguments:
- edges_in: bfloat16 [2, 2, 2, 4096, 768], P('section', None, None, ('dp', 'tensor')), may hold values from -6 to 6
- joint_weight: bfloat16 [2, 2, 3, 768, 768], P('section', None, None, None, 'tensor'), may hold values from -0.21875 to 0.21875
- output_weight: bfloat16 [2, 2, 768, 768], P('section', None, 'tensor'), may hold values from -0.625 to 0.625
- lift_weight: bfloat16 [2, 2, 768, 3072], P('section', None, None, 'tensor'), may hold values from -0.21875 to 0.21875
- lift_bias: bfloat16 [2, 2, 3072], P('section', None, 'tensor'), may hold values from -3 to 3
- drop_weight: bfloat16 [2, 2, 3072, 768], P('section', None, 'tensor'), may hold values from -0.15625 to 0.15625
- norm_gains: bfloat16 [2, 2, 2, 768], P('section'), may hold values from 0.25 to 1.75
- norm_shifts: bfloat16 [2, 2, 2, 768], P('section'), may hold values from -2 to 2
- branch_biases: bfloat16 [2, 2, 2, 768], P('section'), may hold values from -2 to 2
- item_lengths: int32 [8, 2, 3], P('dp'), may hold values from 0 to 400, as said below
- key_keep: int32 [8, 2, 512], P('dp'), may hold values 0 or 1
Outputs:
- edges_out: bfloat16 [2, 2, 2, 4096, 768], P('section', None, None, ('dp', 'tensor'))
- grad_joint: float32 [2, 2, 3, 768, 768], P('section', None, None, None, 'tensor')
- grad_output: float32 [2, 2, 768, 768], P('section', None, 'tensor')
- grad_lift: float32 [2, 2, 768, 3072], P('section', None, None, 'tensor')
- grad_lift_bias: float32 [2, 2, 3072], P('section', None, 'tensor')
- grad_drop: float32 [2, 2, 3072, 768], P('section', None, 'tensor')
- grad_gains: float32 [2, 2, 2, 768], P('section')
- grad_shifts: float32 [2, 2, 2, 768], P('section')
- grad_biases: float32 [2, 2, 2, 768], P('section')
The draws below stay inside these ranges and needn't reach their ends.
Inputs may be any that keep to these rules, and one draw needn't show every extreme that they name: `item_lengths`: each entry is 0, 144, 225 or 400; within a pack the nonzero entries come first and sum to at most 512.
All inputs are finite; a program needn't handle non-finite values. No bound on the sum of `key_keep` on one device may be relied on, other than what follows from the above.
Results may differ from the reference program's by a relative error of at most 0.02.
Values may be sent and summed in bfloat16 or wider, within the bound.
A program may use at most 320 MiB of HBM per device.

```python
import jax
import jax.numpy as jnp
from jax import lax

D = 768
HEADS = 12
HEAD_DIM = 64
FF = 3072
MB = 2
TOK_MB = 512
ITEMS = 3
GROUPS = 8
TOKENS = 4096


def draw_item_lengths(key, part):
    key = jax.random.fold_in(key, 11)
    kinds = jax.random.randint(key, (GROUPS, MB, ITEMS), 0, 3)
    kinds = kinds.at[0, 0, 0].set(2)
    table = jnp.array([144, 225, 400], dtype=jnp.int32)
    lengths = table[kinds]
    running = jnp.cumsum(lengths, axis=-1)
    return jnp.where(running <= TOK_MB, lengths, 0).astype(jnp.int32)


def plant(entries, key, least, high):
    spot = [jax.random.randint(jax.random.fold_in(key, axis), (), 0, length) for axis, length in enumerate(entries.shape)]
    main_axis = entries.shape.index(max(entries.shape))
    next_to = spot[:main_axis] + [(spot[main_axis] + 1) % entries.shape[main_axis]] + spot[main_axis + 1:]
    return entries.at[tuple(spot)].set(least).at[tuple(next_to)].set(high)


def steps_of(rng, extent, cuts, least, high):
    def one(dim, blocks):
        draws = jax.random.uniform(jax.random.fold_in(jax.random.fold_in(rng, 6), dim), (blocks,), jnp.float32, least / len(cuts), high / len(cuts))
        return jnp.repeat(jnp.exp(draws), extent[dim] // blocks).reshape((-1,) + (1,) * (len(extent) - dim - 1))

    gain = one(*cuts[0])
    for cut in cuts[1:]:
        gain = gain * one(*cut)
    return gain


def noise(own_key, dims, deviation, reach, cuts=(), held_as=jnp.bfloat16):
    values = deviation * jax.random.normal(own_key, dims, jnp.float32)
    if cuts:
        values = values * steps_of(own_key, dims, cuts, -0.22, 0.18)
    return jnp.clip(values, -reach, reach).astype(held_as)


def setup_inputs(seed: int = 0) -> dict:
    key_of = jax.random.split(jax.random.key(seed), 12)
    return {
        "edges_in": noise(key_of[0], (2, 2, MB, TOKENS, D), 1.0, 6.0, ((0, 2), (3, 16))),
        "joint_weight": noise(key_of[1], (2, 2, 3, D, D), D ** -0.5, 0.21875, ((0, 2), (4, 2))),
        "output_weight": noise(key_of[2], (2, 2, D, D), (D // 8) ** -0.5, 0.625, ((0, 2), (2, 2))),
        "lift_weight": noise(key_of[3], (2, 2, D, FF), D ** -0.5, 0.21875, ((0, 2), (3, 2))),
        "lift_bias": noise(key_of[4], (2, 2, FF), 0.5, 3.0, ((0, 2), (2, 2))),
        "drop_weight": noise(key_of[5], (2, 2, FF, D), (FF // 2) ** -0.5, 0.15625, ((0, 2), (2, 2))),
        "norm_gains": jnp.clip(1.0 + 0.15 * jax.random.normal(key_of[6], (2, 2, 2, D), jnp.float32), 0.25, 1.75).astype(jnp.bfloat16),
        "norm_shifts": noise(key_of[7], (2, 2, 2, D), 0.3, 2.0, ((0, 2),)),
        "branch_biases": noise(key_of[8], (2, 2, 2, D), 0.3, 2.0, ((0, 2),)),
        "item_lengths": draw_item_lengths(jax.random.fold_in(key_of[11], 71), 0),
        "key_keep": plant((jax.random.randint(key_of[10], (GROUPS, MB, TOK_MB), 0, 4) < 3).astype(jnp.int32), jax.random.fold_in(key_of[10], 1), 0, 1),
    }


EPSILON = 1e-06
HIGHEST = lax.Precision.HIGHEST

@jax.custom_vjp
def low(v):
    return lax.optimization_barrier(v.astype(jnp.bfloat16)).astype(jnp.float32)

@jax.custom_vjp
def low_back(v):
    return v

def low_keep(v):
    return (low(v), None)

def low_pass(kept, grad):
    return (grad,)

def back_keep(v):
    return (v, None)

def back_low(kept, grad):
    return (low(grad),)
low.defvjp(low_keep, low_pass)
low_back.defvjp(back_keep, back_low)

def geometry(lengths, keep_row):
    rows_all = keep_row.shape[0]
    slots = lengths.shape[0]
    positions = jnp.arange(rows_all, dtype=jnp.int32)
    item_ends = jnp.cumsum(lengths).astype(jnp.int32)
    segment = lax.optimization_barrier(jnp.sum((positions[:, None] >= item_ends[None, :]).astype(jnp.int32), axis=1))
    following = jnp.arange(1, slots + 1, dtype=jnp.int32)
    item_ids = jnp.arange(slots, dtype=jnp.int32)
    begin = lax.optimization_barrier(jnp.sum(jnp.where(segment[:, None] == following[None, :], item_ends[None, :], 0), axis=1))
    length = lax.optimization_barrier(jnp.sum(jnp.where(segment[:, None] == item_ids[None, :], lengths[None, :], 0), axis=1))
    grid_side = jnp.where(length == 144, 12, jnp.where(length == 225, 15, 20)).astype(jnp.int32)
    offset = positions - begin
    grid_row = (offset // grid_side).astype(jnp.float32)
    column = (offset % grid_side).astype(jnp.float32)
    row_gap = grid_row[:, None] - grid_row[None, :]
    col_gap = column[:, None] - column[None, :]
    distance = jnp.sqrt(row_gap * row_gap + col_gap * col_gap)
    allowed = (segment[:, None] == segment[None, :]) & ((keep_row[None, :] == 1) | (positions[:, None] == positions[None, :]))
    return (allowed, distance)

def normalize(values_in, gain_vec, shift_vec):
    row_mean = lax.optimization_barrier(jnp.mean(values_in, axis=-1, keepdims=True))
    centred = values_in - row_mean
    variance = lax.optimization_barrier(jnp.mean(centred * centred, axis=-1, keepdims=True))
    return centred * lax.rsqrt(variance + EPSILON) * gain_vec + shift_vec

def run_layer(params, inputs, is_cross, allowed, distance, slopes):
    joint_weight, output_weight, lift_weight, lift_bias, drop_weight, norm_gains, norm_shifts, branch_biases = params
    rows_all = inputs.shape[1]
    normed = low(normalize(inputs, norm_gains[:, 0][:, None, :], norm_shifts[:, 0][:, None, :]))
    source = jnp.stack([normed[0], normed[0]]) if is_cross else normed
    queries = low(HEAD_DIM ** (-0.5) * low_back(jnp.einsum('bnd,bde->bne', normed, joint_weight[:, 0], precision=HIGHEST)))
    keys_low = low(low_back(jnp.einsum('bnd,bde->bne', source, joint_weight[:, 1], precision=HIGHEST)))
    values_low = low(low_back(jnp.einsum('bnd,bde->bne', source, joint_weight[:, 2], precision=HIGHEST)))
    query_heads = queries.reshape(2, rows_all, HEADS, HEAD_DIM)
    key_heads = keys_low.reshape(2, rows_all, HEADS, HEAD_DIM)
    value_heads = values_low.reshape(2, rows_all, HEADS, HEAD_DIM)
    scores = jnp.einsum('bqhe,bkhe->bhqk', query_heads, key_heads, precision=HIGHEST)
    scores = scores - slopes[None, :, None, None] * distance[None, None]
    scores = low_back(jnp.where(allowed[None, None], scores, -1000000000.0))
    shifted = scores - lax.optimization_barrier(jnp.max(scores, axis=-1, keepdims=True))
    expo = jnp.exp(shifted)
    softmax_probs = expo / lax.optimization_barrier(jnp.sum(expo, axis=-1, keepdims=True))
    context = jnp.einsum('bhqk,bkhe->bqhe', low(softmax_probs), value_heads, precision=HIGHEST).reshape(2, rows_all, D)
    context = low_back(low(context))
    attended = low_back(jnp.einsum('bnd,bde->bne', context, output_weight, precision=HIGHEST) + branch_biases[:, 0][:, None, :])
    middle = inputs + attended
    mixed_low = low(normalize(middle, norm_gains[:, 1][:, None, :], norm_shifts[:, 1][:, None, :]))
    hidden = low_back(jnp.einsum('bnd,bdf->bnf', mixed_low, lift_weight, precision=HIGHEST) + lift_bias[:, None, :])
    active = low(jax.nn.gelu(hidden, approximate=False))
    return middle + jnp.einsum('bnf,bfd->bnd', active, drop_weight, precision=HIGHEST) + branch_biases[:, 1][:, None, :]

def reference(edges_in, joint_weight, output_weight, lift_weight, lift_bias, drop_weight, norm_gains, norm_shifts, branch_biases, item_lengths, key_keep):
    params = tuple((arr.astype(jnp.float32) for arr in (joint_weight, output_weight, lift_weight, lift_bias, drop_weight, norm_gains, norm_shifts, branch_biases)))
    pack_count = GROUPS * MB
    blocks = edges_in.reshape(2, 2, MB, GROUPS, TOK_MB, D).transpose(3, 2, 0, 1, 4, 5).reshape(pack_count, 2, 2, TOK_MB, D)
    lengths_all = item_lengths.reshape(pack_count, ITEMS)
    keep_rows = key_keep.reshape(pack_count, TOK_MB)
    slopes = jnp.power(2.0, -8.0 * jnp.arange(1, HEADS + 1, dtype=jnp.float32) / HEADS)

    def one_pack(totals, inputs):
        pack_data, lengths_row, keep_row = inputs
        allowed, distance = geometry(lengths_row, keep_row)

        def both_layers(weights, start_rows):
            first_out = run_layer(tuple((arr[0] for arr in weights)), start_rows, False, allowed, distance, slopes)
            passed = low_back(low(first_out))
            return run_layer(tuple((arr[1] for arr in weights)), passed, True, allowed, distance, slopes)
        joined_rows, pull_back = jax.vjp(both_layers, params, pack_data[0].astype(jnp.float32))
        weight_grads, input_grad = pull_back(pack_data[1].astype(jnp.float32))
        totals = jax.tree.map(lambda former, latter: former + latter, totals, weight_grads)
        return (totals, (input_grad.astype(jnp.bfloat16), joined_rows.astype(jnp.bfloat16)))
    empty_grads = tuple((jnp.zeros(arr.shape, jnp.float32) for arr in params))
    totals, (input_grads, joined_rows) = lax.scan(one_pack, empty_grads, (blocks, lengths_all, keep_rows))
    edges = jnp.stack([input_grads, joined_rows], axis=1)
    edges = edges.reshape(GROUPS, MB, 2, 2, TOK_MB, D).transpose(2, 3, 1, 0, 4, 5).reshape(2, 2, MB, TOKENS, D)
    return (edges, totals[0], totals[1], totals[2], totals[3], totals[4], totals[5], totals[6], totals[7])
```

```python
from functools import partial

import jax
import jax.numpy as jnp
from jax import lax
from jax.experimental import pallas as pl
from jax.experimental.pallas import tpu as pltpu
from jax.sharding import PartitionSpec as P

HEADS = 12
HEAD_DIM = 64
EPSILON = 1e-06
SCALE = HEAD_DIM ** (-0.5)
FAR = 1e30
CHUNK = 32
AHEAD = 3
HOP = 2
VMEM_LIMIT = 44 * 1024 * 1024
MESH = pl.DeviceIdType.MESH


def swap(value, axis):
    return lax.ppermute(value, axis, [(0, 1), (1, 0)])


def pick(stacked, index, axis=0):
    return lax.dynamic_index_in_dim(stacked, index, axis, keepdims=False)


def masked_distance(lengths, keep_row):
    rows_all = keep_row.shape[0]
    slots = lengths.shape[0]
    positions = jnp.arange(rows_all, dtype=jnp.int32)
    ends = jnp.cumsum(lengths)
    segment = jnp.sum((positions[:, None] >= ends[None, :]).astype(jnp.int32), axis=1)
    following = jnp.arange(1, slots + 1, dtype=jnp.int32)
    item_ids = jnp.arange(slots, dtype=jnp.int32)
    begin = jnp.sum(jnp.where(segment[:, None] == following[None, :], ends[None, :], 0), axis=1)
    length = jnp.sum(jnp.where(segment[:, None] == item_ids[None, :], lengths[None, :], 0), axis=1)
    side = jnp.where(length == 144, 12, jnp.where(length == 225, 15, 20)).astype(jnp.int32)
    offset = positions - begin
    grid_row = (offset // side).astype(jnp.float32)
    column = (offset % side).astype(jnp.float32)
    row_gap = grid_row[:, None] - grid_row[None, :]
    col_gap = column[:, None] - column[None, :]
    distance = jnp.sqrt(row_gap * row_gap + col_gap * col_gap)
    allowed = (segment[:, None] == segment[None, :]) & (
        (keep_row[None, :] == 1) | (positions[:, None] == positions[None, :])
    )
    return jnp.where(allowed, distance, FAR)


def dot(a, b, dims=((1,), (0,))):
    return lax.dot_general(a, b, (dims, ((), ())), preferred_element_type=jnp.float32)


def low(value):
    return value.astype(jnp.bfloat16)


def wide(value):
    return value.astype(jnp.float32)


def shape(dims, dtype=jnp.bfloat16):
    return jax.ShapeDtypeStruct(tuple(dims), dtype)


def row_blocks(count, size=64):
    return [pl.ds(r, size) for r in range(0, count, size)]


def norm_rows(values, gain, shift):
    mean = jnp.mean(values, axis=-1, keepdims=True)
    centred = values - mean
    variance = jnp.mean(centred * centred, axis=-1, keepdims=True)
    return centred * lax.rsqrt(variance + EPSILON) * gain + shift


def norm_rows_back(values, grad, gain):
    mean = jnp.mean(values, axis=-1, keepdims=True)
    centred = values - mean
    variance = jnp.mean(centred * centred, axis=-1, keepdims=True)
    spread = lax.rsqrt(variance + EPSILON)
    unit = centred * spread
    scaled = grad * gain
    along = jnp.mean(scaled * unit, axis=-1, keepdims=True)
    level = jnp.mean(scaled, axis=-1, keepdims=True)
    return spread * (scaled - level - unit * along), grad * unit


def column_sum(value):
    return jnp.sum(value, axis=0, keepdims=True)


def widen_kernel(g_ref, drop, lift, joint, out):
    number = pl.program_id(1)
    part = joint.shape[-1]
    count = pl.num_programs(1)

    @pl.when(number < (count - 2) // 2)
    def _():
        drop[...] = wide(g_ref[...])

    @pl.when((number >= (count - 2) // 2) & (number < count - 2))
    def _():
        lift[...] = wide(g_ref[...])

    @pl.when(number == count - 2)
    def _():
        for i in range(2):
            joint[0, i] = wide(g_ref[0, :, pl.ds(i * part, part)])

    @pl.when(number == count - 1)
    def _():
        for i in range(2):
            joint[0, 2, pl.ds(i * part, part)] = wide(g_ref[0, pl.ds(0, part), pl.ds(i * part, part)])
        out[0] = wide(g_ref[0, pl.ds(part, part)])


def widened(grads, inner, part):
    streams, _, width = grads.shape
    each = inner // width
    block = (1, width, width)
    return pl.pallas_call(
        widen_kernel,
        grid=(streams, 2 * each + 2),
        in_specs=[pl.BlockSpec(block, lambda b, i: (b, i, 0))],
        out_specs=[
            pl.BlockSpec(block, lambda b, i: (b, jnp.minimum(i, each - 1), 0)),
            pl.BlockSpec(block, lambda b, i: (b, 0, jnp.clip(i - each, 0, each - 1))),
            pl.BlockSpec((1, 3, width, part), lambda b, i: (b, 0, 0, 0)),
            pl.BlockSpec((1, part, width), lambda b, i: (b, 0, 0)),
        ],
        out_shape=[
            shape((streams, inner, width), jnp.float32),
            shape((streams, width, inner), jnp.float32),
            shape((streams, 3, width, part), jnp.float32),
            shape((streams, part, width), jnp.float32),
        ],
        compiler_params=pltpu.CompilerParams(vmem_limit_bytes=VMEM_LIMIT),
    )(grads)


class Names:
    def __init__(self, pairs):
        for name, ref in pairs:
            setattr(self, name, ref)


KEPT = ("qkvc", "e", "inv", "normed", "source", "middle", "mixed", "act", "steep", "base")
WEIGHTS = ("drop", "lift", "joint", "out")
GIVEN = ("joint", "out", "small", "lift", "drop")
VECTORS = 6
LOADS = 64


def kept_shapes(s, packs, every, width, part, inner):
    heads = part // HEAD_DIM
    f32 = jnp.float32
    dims = {
        "qkvc": shape((packs, every, 4 * part)),
        "e": shape((packs, heads, every, every)),
        "inv": shape((packs, every, part), f32),
        "normed": shape((packs, every, width)),
        "source": shape((packs, every, width)),
        "middle": shape((packs, every, width), f32),
        "mixed": shape((packs, every, width)),
        "act": shape((packs, every, inner)),
        "steep": shape((packs, every, inner)),
        "base": shape((packs, every, width)),
    }
    if s == 0:
        dims.pop("source")
    return dims


def forward_plan(packs, every, width, part, inner):
    full, f32, bf16 = (packs, every, width), jnp.float32, jnp.bfloat16
    rooms = {
        "joint": ((2, 3, width, part), bf16),
        "out": ((2, part, width), bf16),
        "small_in": ((2, 16, width), bf16),
        "lift": ((2, width, inner), bf16),
        "drop": ((2, inner, width), bf16),
        "dist": ((packs, every, every), f32),
        "rows_in": (full, bf16),
        "base": (full, bf16),
        "dy": (full, bf16),
        "normed": (full, bf16),
        "crossed": (full, bf16),
        "source": (full, bf16),
        "qkvc": ((packs, every, 4 * part), bf16),
        "e": ((part // HEAD_DIM, every, every), bf16),
        "inv": ((packs, every, part), f32),
        "a_mine": (full, bf16),
        "a_peer": (full, bf16),
        "y_mine": (full, bf16),
        "y_peer": (full, bf16),
        "middle": (full, f32),
        "mixed": (full, bf16),
        "act": ((packs, every, inner), bf16),
        "steep": ((packs, every, inner), bf16),
        "scores": ((2, every, every), f32),
        "hidden": ((2, every, 256), f32),
    }
    sem = pltpu.SemaphoreType.DMA
    flags = {
        "w_load": sem((5,)),
        "w_send": sem((5,)),
        "w_recv": sem((5,)),
        "d_load": sem((packs,)),
        "r_load": sem((2, packs)),
        "r_send": sem((2, 2, 2, packs)),
        "r_recv": sem((2, 2, packs)),
        "x_send": sem((2, 2, packs)),
        "x_recv": sem((2, 2, packs)),
        "c_send": sem((packs,)),
        "c_recv": sem((packs,)),
        "store": sem((LOADS,)),
    }
    scratch = [pltpu.VMEM(*spec) for spec in rooms.values()] + list(flags.values())
    return list(rooms) + list(flags), scratch


def forward_kernel(packs, names, *refs):
    refs = list(refs)

    def take(n):
        taken = refs[:n]
        del refs[:n]
        return taken

    slopes, rows_ref, dist_ref = take(3)
    given = dict(zip(GIVEN, take(5)))
    kept = [
        Names(zip([k for k in KEPT if s or k != "source"], take(len(KEPT) - (s == 0)))) for s in range(2)
    ]
    placed = [Names(zip(WEIGHTS, take(4))) for _ in range(2)]
    small_ref, dy_ref, y_ref = take(3)
    w = Names(zip(names, refs))
    core, half = lax.axis_index("section"), lax.axis_index("tensor")
    away = 1 - half
    every, width = w.base.shape[1:]
    rows = every // 2
    part, inner = w.out.shape[1], w.drop.shape[1]
    own = pl.ds(pl.multiple_of(half * rows, rows), rows)
    x_peer = {"tensor": away}
    sibling = {"section": 1 - core}
    early = lax.broadcasted_iota(jnp.int32, (1, 2 * HEAD_DIM), 1) < HEAD_DIM
    across = ((1,), (1,))

    def remote(src, dst, sent, got, target):
        return pltpu.make_async_remote_copy(
            src_ref=src, dst_ref=dst, send_sem=sent, recv_sem=got,
            device_id=target, device_id_type=MESH,
        )

    def weight_load(i):
        return pltpu.make_async_copy(
            given[GIVEN[i]].at[core], getattr(w, room[i]).at[core], w.w_load.at[i]
        )

    def weight_out(i):
        return remote(
            given[GIVEN[i]].at[1 - core], getattr(w, room[i]).at[core], w.w_send.at[i], w.w_recv.at[i], sibling
        )

    def dist_load(m):
        return pltpu.make_async_copy(dist_ref.at[m], w.dist.at[m], w.d_load.at[m])

    room = ("joint", "out", "small_in", "lift", "drop")
    lands = (w.rows_in, w.dy)

    def rows_load(kind, m):
        return pltpu.make_async_copy(rows_ref.at[kind, m], lands[kind].at[m, own], w.r_load.at[kind, m])

    def rows_out(kind, b, t, m):
        side = jnp.where(t == half, 0, 1)
        return remote(
            rows_ref.at[b, m], lands[kind].at[m, own], w.r_send.at[kind, b, side, m], w.r_recv.at[kind, side, m],
            {"section": b, "tensor": t},
        )

    def rows_start(kind, m):
        @pl.when(core == kind)
        def _():
            rows_out(kind, 1 - kind, away, m).start()
            rows_out(kind, kind, away, m).start()
            rows_out(kind, 1 - kind, half, m).start()

    def rows_got(kind, m):
        rows_out(kind, 0, away, m).wait_recv()

        @pl.when(core == kind)
        def _():
            rows_load(kind, m).wait()

        @pl.when(core != kind)
        def _():
            rows_out(kind, 0, half, m).wait_recv()

    def rows_sent(kind, m):
        @pl.when(core == kind)
        def _():
            rows_out(kind, 1 - kind, away, m).wait_send()
            rows_out(kind, kind, away, m).wait_send()
            rows_out(kind, 1 - kind, half, m).wait_send()

    for i in range(len(room)):
        weight_load(i).start()
    for m in range(packs):
        dist_load(m).start()
        for kind in range(2):
            pl.when(core == kind)(lambda: rows_load(kind, m).start())
    barrier = pltpu.get_barrier_semaphore()
    for c, t in [(1 - core, half), (core, away), (1 - core, away)]:
        pl.semaphore_signal(
            barrier, inc=1, device_id={"section": c, "tensor": t}, device_id_type=MESH
        )
    pl.semaphore_wait(barrier, 3)
    rows_start(0, 0)
    for i in range(3):
        weight_out(i).start()
    for m in range(1, packs):
        rows_start(0, m)
    for i in range(3, len(room)):
        weight_out(i).start()

    numbers = iter(range(LOADS))
    pending = {}

    def store(key, src, dst):
        copy = pltpu.make_async_copy(src, dst, w.store.at[next(numbers)])
        copy.start()
        pending[key] = copy

    def free(*key):
        if key in pending:
            pending.pop(key).wait()

    def keep(name, s, m):
        store((name, m), getattr(w, name).at[m], getattr(kept[s], name).at[m])

    def weight_got(name, s):
        i = room.index(name)
        pl.when(core == s)(lambda: weight_load(i).wait())
        pl.when(core != s)(lambda: weight_out(i).wait_recv())
        if name in WEIGHTS:
            store((name, "placed", s), getattr(w, name).at[s], getattr(placed[s], name))

    vectors = [None, None]

    def small_got(s):
        weight_got("small_in", s)
        vectors[s] = wide(w.small_in[s])
        small_ref[s] = vectors[s]

    def row(s, i):
        return vectors[s][i : i + 1]

    def over_x(src, dst, kind, s, m):
        return remote(src, dst, w.x_send.at[kind, s, m], w.x_recv.at[kind, s, m], x_peer)

    def a_copy(s, m):
        return over_x(w.a_mine.at[m], w.a_peer.at[m], 0, s, m)

    def y_copy(m):
        return over_x(w.y_mine.at[m], w.y_peer.at[m], 1, 0, m)

    def crossing(m):
        return remote(w.normed.at[m], w.crossed.at[m], w.c_send.at[m], w.c_recv.at[m], sibling)

    def attention(s, m):
        source = w.source if s else w.normed
        free("qkvc", m)
        w.qkvc[m, :, pl.ds(0, part)] = low(SCALE * dot(w.normed[m], w.joint[s, 0]))
        if s:

            @pl.when(core == 0)
            def _():
                w.source[m] = w.normed[m]

            @pl.when(core == 1)
            def _():
                crossing(m).wait_recv()
                w.source[m] = w.crossed[m]

            keep("source", s, m)
        for i in (1, 2):
            w.qkvc[m, :, pl.ds(i * part, part)] = low(dot(source[m], w.joint[s, i]))
        if s == 0:
            dist_load(m).wait()
        free("inv", m)
        free("e")

        @pl.loop(0, part // (2 * HEAD_DIM))
        def _(pair):
            def lanes(i):
                start = i * part + pair * 2 * HEAD_DIM
                return pl.ds(pl.multiple_of(start, 2 * HEAD_DIM), 2 * HEAD_DIM)

            queries, keys, values = (w.qkvc[m, :, lanes(i)] for i in range(3))
            for side in range(2):
                here = early if side == 0 else jnp.logical_not(early)
                w.scores[side] = dot(jnp.where(here, queries, 0), keys, across)
            for side in range(2):
                head = 2 * pair + side
                here = early if side == 0 else jnp.logical_not(early)
                slope = slopes[head]
                for at in row_blocks(every):
                    value = w.scores[side, at] - slope * w.dist[m, at]
                    expo = jnp.exp(value - jnp.max(value, axis=-1, keepdims=True))
                    w.e[head, at] = low(expo)
                    inverse = 1.0 / jnp.sum(expo, axis=-1, keepdims=True)
                    if side == 0:
                        w.inv[m, at, lanes(0)] = jnp.broadcast_to(inverse, (64, 2 * HEAD_DIM))
                    else:
                        w.inv[m, at, lanes(0)] = jnp.where(here, inverse, w.inv[m, at, lanes(0)])
            sums = [dot(w.e[2 * pair + side], values) for side in range(2)]
            context = jnp.where(early, sums[0], sums[1]) * w.inv[m, :, lanes(0)]
            w.qkvc[m, :, lanes(3)] = low(context)

        if m == 0:
            weight_got("out", s)
        if s:
            a_copy(0, m).wait_send()
        for r in (0, rows):
            at = pl.ds(r, rows)
            w.a_mine[m, at] = low(dot(w.qkvc[m, at, pl.ds(3 * part, part)], w.out[s]))
        a_copy(s, m).start()
        store(("e",), w.e, kept[s].e.at[m])
        keep("qkvc", s, m)
        keep("inv", s, m)

    def feed_forward(s, m):
        base = w.base if s else w.rows_in
        a_copy(s, m).wait_recv()
        for name in ("middle", "mixed", "act", "steep"):
            free(name, m)
        for at in row_blocks(every):
            total = wide(w.a_mine[m, at]) + wide(w.a_peer[m, at])
            value = wide(base[m, at]) + total + row(s, 4)
            w.middle[m, at] = value
            w.mixed[m, at] = low(norm_rows(value, row(s, 1), row(s, 3)))
        if m == 0:
            weight_got("lift", s)
            weight_got("drop", s)
        size = w.hidden.shape[-1]
        for number in range(inner // size):
            lanes = pl.ds(number * size, size)
            at, off = divmod(number * size, width)
            bias = vectors[s][VECTORS + at : VECTORS + at + 1, off : off + size]
            w.hidden[number % 2] = dot(w.mixed[m], w.lift[s, :, lanes])
            for at in row_blocks(every):
                value = w.hidden[number % 2, at] + bias
                below = 0.5 + 0.5 * lax.erf(value * (0.5**0.5))
                density = 0.3989422804014327 * jnp.exp(-0.5 * value * value)
                w.act[m, at, lanes] = low(value * below)
                w.steep[m, at, lanes] = low(below + value * density)
        if s:
            y_copy(m).wait_send()
        for r in (0, rows):
            at = pl.ds(r, rows)
            w.y_mine[m, at] = low(dot(w.act[m, at], w.drop[s]))
        if s == 0:
            y_copy(m).start()
        else:
            store(("y", m), w.y_mine.at[m], y_ref.at[m])
        for name in ("middle", "mixed", "act", "steep"):
            keep(name, s, m)

    def enter(m):
        y_copy(m).wait_recv()
        free("normed", m)
        for at in row_blocks(every):
            total = wide(w.y_mine[m, at]) + wide(w.y_peer[m, at])
            value = low(w.middle[m, at] + total + row(0, 5))
            w.base[m, at] = value
            w.normed[m, at] = low(norm_rows(wide(value), row(1, 0), row(1, 2)))
        pl.when(core == 0)(lambda: crossing(m).start())
        keep("base", 1, m)
        keep("normed", 1, m)

    small_got(0)
    weight_got("joint", 0)
    for m in range(packs):
        rows_got(0, m)
        for at in row_blocks(every):
            w.normed[m, at] = low(norm_rows(wide(w.rows_in[m, at]), row(0, 0), row(0, 2)))
        store(("rows", m), w.rows_in.at[m], kept[0].base.at[m])
        keep("normed", 0, m)
        attention(0, m)
    for m in range(packs):
        feed_forward(0, m)
    small_got(1)
    weight_got("joint", 1)
    for m in range(packs):
        enter(m)
        attention(1, m)
    for m in range(packs):
        rows_start(1, m)
    for m in range(packs):
        feed_forward(1, m)
    for m in range(packs):
        rows_got(1, m)
        store(("dy", m), w.dy.at[m], dy_ref.at[m])
    for i in range(len(room)):
        weight_out(i).wait_send()
    for m in range(packs):
        for kind in range(2):
            rows_sent(kind, m)
        a_copy(1, m).wait_send()
        pl.when(core == 0)(lambda: crossing(m).wait_send())
    for key in list(pending):
        free(*key)


def forward(slopes, held, distances, weights):
    packs, rows, width = held.shape[1:]
    every = 2 * rows
    part, inner = weights[1].shape[1], weights[4].shape[1]
    order = dict(zip(GIVEN, weights))
    kept = [kept_shapes(s, packs, every, width, part, inner) for s in range(2)]
    outs = list(kept[0].values()) + list(kept[1].values())
    outs += [shape(order[name].shape[1:]) for name in WEIGHTS] * 2
    outs += [shape((2, 16, width), jnp.float32), shape((packs, every, width)), shape((packs, every, width))]
    names, scratch = forward_plan(packs, every, width, part, inner)
    anywhere = pl.BlockSpec(memory_space=pl.ANY)
    out_specs = [anywhere] * len(outs)
    out_specs[-3] = pl.BlockSpec(memory_space=pltpu.VMEM)
    found = list(
        pl.pallas_call(
            partial(forward_kernel, packs, names),
            out_shape=outs,
            in_specs=[pl.BlockSpec(memory_space=pltpu.SMEM)] + [anywhere] * 7,
            out_specs=out_specs,
            scratch_shapes=scratch,
            compiler_params=pltpu.CompilerParams(
                collective_id=1, has_side_effects=True, vmem_limit_bytes=60 * 1024 * 1024
            ),
        )(slopes, held, distances, *weights)
    )
    results = []
    for s in range(2):
        layer = {name: found.pop(0) for name in kept[s]}
        layer.setdefault("source", layer["normed"])
        results.append([layer[name] for name in KEPT])
    placed = [[found.pop(0) for _ in WEIGHTS] for _ in range(2)]
    return results, placed, *found


def reducer(line, count, g_refs, o_ref, bufs, sems):
    load_ring, loads_ring, from_y, from_prv, from_nxt, both, mid2, from_y2, res2 = bufs
    load_sem, y_send, y_recv, n_send, n_recv, p_send, p_recv, f_send = sems[:8]
    load2, n2_send, p2_recv, m2_recv, u2_send, u2_recv, a2_send, r2_recv, o2_send = sems[8:17]
    s_send, l_sem, s2_send, l2_sem, f_recv, d_recv, s_recv = sems[17:]
    dp = lax.axis_index("dp")
    core = lax.axis_index("section")
    y, z = dp % 2, dp // 2
    depth = line // 2 - 1
    left = z < line // 2
    step = jnp.where(left, 1, -1)
    edge = jnp.where(left, z, line - 1 - z)
    mine = jnp.where(left, 0, 1)
    total = 2 * count
    slots = from_y.shape[0]
    ring = load_ring.shape[0]
    inner = edge == depth
    outer = jnp.logical_not(inner)

    def device(z_at, y_at, core_at):
        return {"dp": z_at * 2 + y_at, "section": core_at}

    across = device(z, 1 - y, core)
    across_other = device(z, 1 - y, 1 - core)
    sibling = device(z, y, 1 - core)
    nxt = device(z + step, y, core)
    prv = device(z - step, y, core)

    def greet(extra):
        barrier = pltpu.get_barrier_semaphore()
        targets = [across, across_other, sibling, nxt] + extra
        for target in targets:
            pl.semaphore_signal(barrier, inc=1, device_id=target, device_id_type=MESH)

        @pl.when(edge > 0)
        def _():
            pl.semaphore_signal(barrier, inc=1, device_id=prv, device_id_type=MESH)

        pl.semaphore_wait(barrier, len(targets) + jnp.where(edge > 0, 1, 0))

    def send(src, dst, sent, got, target):
        return pltpu.make_async_remote_copy(
            src_ref=src,
            dst_ref=dst,
            send_sem=sent,
            recv_sem=got,
            device_id=target,
            device_id_type=MESH,
        )

    def plus(into, other):
        return (into.astype(jnp.float32) + other.astype(jnp.float32)).astype(into.dtype)

    def guarded(k, body):
        pl.when((k >= 0) & (k < total))(lambda: body(k))

    def by_layer(k, body):
        pl.when(k < count)(lambda: body(g_refs[1], k))
        pl.when(k >= count)(lambda: body(g_refs[0], k - count))

    def stays(k):
        return jnp.where(k < count, 1, 0) == core

    def place(k):
        return jnp.where(k < count, k, k - count)

    def load(k, g_ref=g_refs[0], j=0):
        return pltpu.make_async_copy(g_ref.at[j, y], load_ring.at[k % ring], load_sem.at[k % ring])

    def over_y(k, g_ref=g_refs[0], j=0):
        i = k % slots
        return send(g_ref.at[j, 1 - y], from_y.at[i], y_send.at[i], y_recv.at[i], across)

    def inward(k):
        i = k % slots
        return send(from_y.at[i], from_prv.at[i], n_send.at[i], p_recv.at[i], nxt)

    def middle(k):
        i = k % slots
        return send(from_y.at[i], from_nxt.at[i], n_send.at[i], n_recv.at[i], nxt)

    def outward(k):
        i = k % slots
        return send(from_nxt.at[i], from_nxt.at[i], p_send.at[i], n_recv.at[i], prv)

    def keep(k):
        i = k % slots
        return pltpu.make_async_copy(from_nxt.at[i], o_ref.at[core, place(k), y], l_sem.at[i])

    def hand(k):
        i = k % slots
        return send(from_nxt.at[i], o_ref.at[core, place(k), y], s_send.at[i], s_recv, sibling)

    def back_same(k):
        i = k % slots
        return send(from_nxt.at[i], o_ref.at[core, place(k), y], f_send.at[i], f_recv, across)

    def back_other(k):
        i = k % slots
        return send(from_nxt.at[i], o_ref.at[core, place(k), y], f_send.at[i], d_recv, across_other)

    def begin(k):
        def one(g_ref, j):
            over_y(k, g_ref, j).start()
            load(k, g_ref, j).start()

        by_layer(k, one)

    def pair(k):
        load(k).wait()
        over_y(k).wait()
        i = k % slots
        from_y[i] = plus(from_y[i], load_ring[k % ring])

    def pass_on(k):
        i = k % slots

        @pl.when(edge > 0)
        def _():
            inward(k).wait_recv()
            from_y[i] = plus(from_y[i], from_prv[i])

        pl.when(inner)(lambda: middle(k).start())
        pl.when(outer)(lambda: inward(k).start())

    def finish(k):
        i = k % slots
        middle(k).wait()

        @pl.when(inner)
        def _():
            from_nxt[i] = plus(from_nxt[i], from_y[i])

        pl.when(edge > 0)(lambda: outward(k).start())

        @pl.when(stays(k))
        def _():
            back_same(k).start()
            keep(k).start()

        @pl.when(jnp.logical_not(stays(k)))
        def _():
            back_other(k).start()
            hand(k).start()

    def loads(k, g_ref=g_refs[0], j=0, into=None):
        into = loads_ring.at[k % ring] if into is None else into
        return pltpu.make_async_copy(g_ref.at[j, pl.ds(2, 2)], into, load2.at[k % ring])

    def inwards(k):
        i = k % slots
        return send(both.at[i], both.at[i], n2_send.at[i], p2_recv.at[i], nxt)

    def halve(k):
        i = k % slots
        return send(both.at[i, 1 - mine], mid2.at[i], n2_send.at[i], m2_recv.at[i], nxt)

    def trade(k):
        i = k % slots
        return send(both.at[i, mine], from_y2.at[i], u2_send.at[i], u2_recv.at[i], across)

    def rejoin(k, q):
        i = k % slots
        return send(res2.at[i, q], res2.at[i, q], a2_send.at[i], r2_recv.at[i, q], nxt)

    def outwards(k, q):
        i = k % slots
        return send(res2.at[i, q], res2.at[i, q], o2_send.at[i, q], r2_recv.at[i, q], prv)

    def keep2(k, q):
        i = k % slots
        return pltpu.make_async_copy(
            res2.at[i, q], o_ref.at[core, place(k), 2 + q], l2_sem.at[i, q]
        )

    def hand2(k, q):
        i = k % slots
        return send(res2.at[i, q], o_ref.at[core, place(k), 2 + q], s2_send.at[i, q], s_recv, sibling)

    def spread(k, q):
        pl.when(edge > 0)(lambda: outwards(k, q).start())
        pl.when(stays(k))(lambda: keep2(k, q).start())
        pl.when(jnp.logical_not(stays(k)))(lambda: hand2(k, q).start())

    def begin2(k):
        def one(g_ref, j):
            pl.when(edge == 0)(lambda: loads(k, g_ref, j, both.at[k % slots]).start())
            pl.when(edge > 0)(lambda: loads(k, g_ref, j).start())

        by_layer(k, one)

    def pass_on2(k):
        i = k % slots
        loads(k).wait()

        @pl.when(edge > 0)
        def _():
            inwards(k).wait_recv()
            both[i] = plus(both[i], loads_ring[k % ring])

        pl.when(inner)(lambda: halve(k).start())
        pl.when(outer)(lambda: inwards(k).start())

    def trade2(k):
        i = k % slots
        halve(k).wait()
        both[i, mine] = plus(both[i, mine], mid2[i])
        trade(k).start()

    def settle2(k):
        i = k % slots
        trade(k).wait()
        res2[i, mine] = plus(both[i, mine], from_y2[i])
        rejoin(k, mine).start()
        spread(k, mine)

    def finish2(k):
        @pl.when(inner)
        def _():
            rejoin(k, 1 - mine).wait_recv()
            spread(k, 1 - mine)

        @pl.when(outer)
        def _():
            inwards(k).wait_send()
            for q in range(2):
                rejoin(k, q).wait_recv()
                spread(k, q)

    def retire(k):
        @pl.when(inner)
        def _():
            rejoin(k, mine).wait_send()

        @pl.when(edge > 0)
        def _():
            outward(k).wait_send()
            for q in range(2):
                outwards(k, q).wait_send()

        back_same(k).wait_send()

        @pl.when(stays(k))
        def _():
            keep(k).wait()
            for q in range(2):
                keep2(k, q).wait()

        @pl.when(jnp.logical_not(stays(k)))
        def _():
            hand(k).wait_send()
            for q in range(2):
                hand2(k, q).wait_send()

    span = AHEAD + HOP * (2 * depth + 3) + 1

    def ticks(first, last):
        @pl.loop(first, last)
        def _(tick):
            now = tick - AHEAD
            guarded(tick - span, retire)
            guarded(tick, begin)
            guarded(now, pair)
            guarded(tick - HOP * edge, begin2)
            guarded(now - HOP * edge, pass_on)
            guarded(now - HOP * edge, pass_on2)

            @pl.when(inner)
            def _():
                guarded(now - HOP * (depth + 1), trade2)
                guarded(now - HOP * (depth + 2), settle2)

            guarded(now - HOP * (2 * depth + 1 - edge), finish)
            guarded(now - HOP * (2 * depth + 3 - edge), finish2)

    def drain():
        group = o_ref.at[0, :, 0]
        groups = o_ref.at[0, :, pl.ds(0, 3)]
        pltpu.make_async_copy(group, group, f_recv).wait()
        pltpu.make_async_copy(group, group, d_recv).wait()
        pltpu.make_async_copy(groups, groups, s_recv).wait()

    return greet, ticks, drain, total + span


def reducer_scratch(line, rows, width):
    slots = AHEAD + HOP * (line + 1) + 3
    ring = AHEAD + 1

    def room(*lead):
        return pltpu.VMEM(lead + (rows, width), jnp.bfloat16)

    def sems(*dims):
        return pltpu.SemaphoreType.DMA(dims)

    bufs = [room(ring), room(ring, 2)] + [room(slots)] * 3 + [room(slots, 2)]
    bufs += [room(slots)] * 2 + [room(slots, 2)]
    many, twice = sems(slots), sems(slots, 2)
    flags = [sems(ring)] + [many] * 7 + [sems(ring)] + [many] * 6 + [twice] * 2
    return bufs, flags + [many] * 2 + [twice] * 2 + [pltpu.SemaphoreType.DMA] * 3


BUFS, SEMS = 9, 24


def reduce_kernel(line, count, g_zero, g_one, o_ref, *refs):
    greet, ticks, drain, length = reducer(
        line, count, (g_zero, g_one), o_ref, refs[:BUFS], refs[BUFS:]
    )
    greet([])
    ticks(0, length)
    drain()


def reduce_over_dp(grads, line):
    count, _, rows, width = grads[0].shape
    bufs, sems = reducer_scratch(line, rows, width)
    return pl.pallas_call(
        partial(reduce_kernel, line, count),
        out_shape=shape((2,) + grads[0].shape),
        in_specs=[pl.BlockSpec(memory_space=pl.ANY)] * 2,
        out_specs=pl.BlockSpec(memory_space=pl.ANY),
        scratch_shapes=bufs + sems,
        compiler_params=pltpu.CompilerParams(
            collective_id=0, has_side_effects=True, vmem_limit_bytes=56 * 1024 * 1024
        ),
    )(*grads)


def backward_scratch(packs, rows, width, part, inner, block):
    full, f32 = (packs, 2 * rows, width), jnp.float32
    bf16 = jnp.bfloat16
    plan = {
        "drop": ((inner, width), bf16),
        "lift": ((width, inner), bf16),
        "joint": ((3, width, part), bf16),
        "out": ((part, width), bf16),
        "dy": (full, bf16),
        "wide_a": ((packs, 2 * rows, inner), bf16),
        "wide_b": ((packs, 2 * rows, inner), bf16),
        "narrow": (full, bf16),
        "source": (full, bf16),
        "dm_mine": (full, bf16),
        "dm_peer": (full, bf16),
        "dn_mine": (full, bf16),
        "dn_peer": (full, bf16),
        "crossed": (full, bf16),
        "middle": (full, f32),
        "dmid": (full, f32),
        "da": (full, bf16),
        "inv": ((packs, 2 * rows, part), f32),
        "base": (full, bf16),
        "ends": ((packs, rows, width), f32),
        "ends_mine": ((packs, rows, width), bf16),
        "ends_peer": ((packs, rows, width), bf16),
        "dx": ((packs, rows, width), bf16),
        "e": ((2, 2, 2 * rows, 2 * rows), bf16),
        "dc": ((2 * rows, part), f32),
        "dprob": ((2, 2 * rows, 2 * rows), f32),
        "ds": ((2, 2 * rows, 2 * rows), bf16),
        "staged": ((3, 2, 4, block // 8, width), bf16),
        "sums": ((2, 8, width), f32),
        "sums_peer": ((2, 8, width), f32),
        "tail": ((4, block // 8, width), bf16),
    }
    sem = pltpu.SemaphoreType.DMA
    flags = {
        "load": sem((LOADS,)),
        "e_load": sem((2,)),
        "x_send": sem((2, 2, packs)),
        "x_recv": sem((2, 2, packs)),
        "c_send": sem((packs,)),
        "c_recv": sem((packs,)),
        "g_store": sem((3,)),
        "t_store": sem((2,)),
        "v_send": sem((2,)),
        "v_recv": sem((2,)),
        "y_send": sem((packs,)),
        "y_recv": sem((packs,)),
        "o_keep": sem((1,)),
        "o_send": sem((1,)),
        "o_recv": sem((1,)),
    }
    return list(plan) + list(flags), [pltpu.VMEM(*spec) for spec in plan.values()] + list(flags.values())


def backward_kernel(line, count, packs, inside, names, *refs):
    refs = list(refs)

    def take(n):
        taken = refs[:n]
        del refs[:n]
        return taken

    small, dy_in, y_in = take(3)
    weights = [Names(zip(WEIGHTS, take(4))) for _ in range(2)]
    kept = [Names(zip(KEPT, take(len(KEPT)))) for _ in range(2)]
    edges_ref, *g_refs = take(3)
    o_ref = take(1)[0] if inside else None
    w = Names(zip(names, take(len(names))))
    core, half = lax.axis_index("section"), lax.axis_index("tensor")
    every, width = w.dy.shape[1:]
    rows = every // 2
    part, inner = w.out.shape[0], w.drop.shape[0]
    block = 8 * w.tail.shape[1]
    pairs = part // (2 * HEAD_DIM)
    x_peer = {"tensor": 1 - half}
    sibling = {"section": 1 - core}
    own = pl.multiple_of(half * rows, rows)
    theirs = pl.multiple_of((1 - half) * rows, rows)
    early = lax.broadcasted_iota(jnp.int32, (1, 2 * HEAD_DIM), 1) < HEAD_DIM
    numbers = iter(range(LOADS))
    down, across = ((0,), (0,)), ((1,), (1,))

    def fetch(src, dst):
        copy = pltpu.make_async_copy(src, dst, w.load.at[next(numbers)])
        copy.start()
        return copy

    def remote(src, dst, sent, got, target):
        return pltpu.make_async_remote_copy(
            src_ref=src, dst_ref=dst, send_sem=sent, recv_sem=got,
            device_id=target, device_id_type=MESH,
        )

    def over_x(src, dst, kind, s, m):
        return remote(src, dst, w.x_send.at[kind, s, m], w.x_recv.at[kind, s, m], x_peer)

    pending = {}

    def ask(key, src, dst):
        pending[key] = fetch(src, dst)

    def got(key):
        pending.pop(key).wait()

    def ask_layer(s):
        for name in ("drop", "lift"):
            ask(name, getattr(weights[s], name), getattr(w, name))

    def ask_rows(s):
        for m in range(packs):
            ask(("steep", m), kept[s].steep.at[m], w.wide_a.at[m])
            ask(("mixed", m), kept[s].mixed.at[m], w.narrow.at[m])

    def ask_attention(s):
        for name in ("joint", "out"):
            ask(name, getattr(weights[s], name), getattr(w, name))
        for m in range(packs):
            ask(("middle", m), kept[s].middle.at[m], w.middle.at[m])
            ask(("inv", m), kept[s].inv.at[m], w.inv.at[m])

    for m in range(packs):
        ask(("dy", m), dy_in.at[m], w.dy.at[m])
        ask(("ends", m), y_in.at[m, pl.ds(own, rows)], w.ends_mine.at[m])
    ask_layer(1)
    ask_rows(1)
    ask_attention(1)

    clock, ready = [0], [0]
    if inside:
        greet, run_ticks, drain, length = reducer(
            line, count, g_refs, o_ref, refs[:BUFS], refs[BUFS:]
        )
        greet([x_peer])

        def ticks(n):
            n = min(n, ready[0] - clock[0])
            if n > 0:
                run_ticks(clock[0], clock[0] + n)
                clock[0] += n
    else:
        barrier = pltpu.get_barrier_semaphore()
        for target in (x_peer, sibling):
            pl.semaphore_signal(barrier, inc=1, device_id=target, device_id_type=MESH)
        pl.semaphore_wait(barrier, 2)

        def ticks(n):
            pass

    def add_sums(s, m, row, value):
        at = pl.ds(row, 1)
        w.sums[s, at] = value if m == 0 else w.sums[s, at] + value

    stores = [None, None, None]
    stored = [0]

    def emit(s, number, fill):
        slot = stored[0] % 3
        stored[0] += 1
        if stores[slot] is not None:
            stores[slot].wait()
        fill(slot)
        stores[slot] = pltpu.make_async_copy(
            w.staged.at[slot], g_refs[s].at[pl.ds(2 * number, 2)], w.g_store.at[slot]
        )
        stores[slot].start()

    def settle_stores():
        for slot in range(3):
            if stores[slot] is not None:
                stores[slot].wait()
                stores[slot] = None

    def put(slot, value, first=0, lanes=slice(None)):
        step = block // 8
        per = 4 * step
        for r in range(0, value.shape[0], step):
            at = first + r
            w.staged[slot, at // per, at % per // step, :, lanes] = low(value[r : r + step])

    def product(lefts, rights):
        return sum(dot(a[...], b[...], down) for a, b in zip(lefts, rights))

    dm = [[over_x(w.dm_mine.at[m], w.dm_peer.at[m], 0, s, m) for m in range(packs)] for s in range(2)]
    dn = [
        [
            over_x(
                w.dn_mine.at[m, pl.ds(theirs, rows)],
                w.dn_peer.at[m, pl.ds(0, rows)],
                1, 0, m,
            )
            for m in range(packs)
        ],
        [over_x(w.dn_mine.at[m], w.dn_peer.at[m], 1, 1, m) for m in range(packs)],
    ]

    def far_copy(m):
        return remote(w.dm_mine.at[m], w.crossed.at[m], w.c_send.at[m], w.c_recv.at[m], sibling)

    def feed_forward(s, m):
        got(("steep", m))
        if s == 0:
            pl.when(core == 1)(lambda: far_copy(m).wait_send())
        size = 256
        for number in range(inner // size):
            lanes = pl.ds(number * size, size)
            grad = dot(w.dy[m], w.drop[lanes], across) * wide(w.wide_a[m, :, lanes])
            grad = low(grad)
            w.wide_b[m, :, lanes] = grad
            total = column_sum(wide(grad))
            at = number * size
            spot = (s, pl.ds(VECTORS + at // width, 1), pl.ds(at % width, size))
            w.sums[spot] = total if m == 0 else w.sums[spot] + total
        ask(("act", m), kept[s].act.at[m], w.wide_a.at[m])
        add_sums(s, m, 5, 0.5 * column_sum(wide(w.dy[m])))
        for r in (0, rows):
            at = pl.ds(r, rows)
            w.dm_mine[m, at] = low(dot(w.wide_b[m, at], w.lift[...], across))
        dm[s][m].start()

    def feed_forward_weights(s, spread):
        for m in range(packs):
            got(("act", m))
            got(("mixed", m))
        number = 0
        for first in range(0, inner, block):
            lanes = pl.ds(first, block)
            value = product([w.wide_a.at[m, :, lanes] for m in range(packs)], [w.dy.at[m] for m in range(packs)])
            emit(s, number, lambda slot: put(slot, value))
            number += 1
            if spread and number % 3 == 0:
                ticks(spread)
        for column in range(0, inner, width):
            for first in range(0, width, block):
                value = product(
                    [w.narrow.at[m, :, pl.ds(first, block)] for m in range(packs)],
                    [w.wide_b.at[m, :, pl.ds(column, width)] for m in range(packs)],
                )
                emit(s, number, lambda slot: put(slot, value))
                number += 1
                if spread and number % 3 == 0:
                    ticks(spread)
        settle_stores()
        ready[0] = (0 if s else count) + 2 * number
        for m in range(packs):
            ask(("qkvc", m), kept[s].qkvc.at[m], w.wide_a.at[m])
            ask(("normed", m), kept[s].normed.at[m], w.narrow.at[m])
            if s:
                ask(("source", m), kept[s].source.at[m], w.source.at[m])
        ask_e(s, 0)

    def e_copy(s, number):
        m, pair = divmod(number, pairs)
        return pltpu.make_async_copy(
            kept[s].e.at[m, pl.ds(2 * pair, 2)], w.e.at[number % 2], w.e_load.at[number % 2]
        )

    def ask_e(s, number):
        if number < packs * pairs:
            e_copy(s, number).start()

    def attention(s, m, spread, between=None):
        if m == 0:
            got("out")
        got(("middle", m))
        if s:
            got(("ends", m))
            for r in range(0, rows, 32):
                at = pl.ds(r, 32)
                mine = w.middle[m, pl.ds(pl.multiple_of(own + r, 32), 32)]
                w.ends[m, at] = mine + wide(w.ends_mine[m, at]) + small[1, pl.ds(5, 1)]
        dm[s][m].wait()
        totals = [0.0, 0.0, 0.0]
        for at in row_blocks(every, 32):
            grad = wide(w.dm_mine[m, at]) + wide(w.dm_peer[m, at])
            pulled, along = norm_rows_back(w.middle[m, at], grad, small[s, pl.ds(1, 1)])
            through = wide(w.dy[m, at]) + pulled
            w.dmid[m, at] = through
            da = low(through)
            w.da[m, at] = da
            for i, piece in enumerate((along, grad, wide(da))):
                totals[i] = totals[i] + column_sum(piece)
        for i, row in enumerate((1, 3, 4)):
            add_sums(s, m, row, 0.5 * totals[i])
        ticks(spread)
        got(("inv", m))
        w.dc[...] = dot(w.da[m], w.out[...], across) * w.inv[m]
        got(("qkvc", m))
        for pair in range(pairs):
            number = m * pairs + pair
            e_copy(s, number).wait()
            ask_e(s, number + 1)
            e_ref = w.e.at[number % 2]

            def lanes(i):
                return pl.ds(i * part + pair * 2 * HEAD_DIM, 2 * HEAD_DIM)

            queries, keys, values = (w.wide_a[m, :, lanes(i)] for i in range(3))
            grad = low(w.dc[:, lanes(0)])
            for side in range(2):
                here = early if side == 0 else jnp.logical_not(early)
                w.dprob[side] = dot(jnp.where(here, grad, 0), values, across)
            for side in range(2):
                here = early if side == 0 else jnp.logical_not(early)
                for at in row_blocks(every):
                    level = jnp.where(here, w.dc[at, lanes(0)] * wide(w.wide_a[m, at, lanes(3)]), 0.0)
                    level = jnp.sum(level, axis=-1, keepdims=True)
                    w.ds[side, at] = low(wide(e_ref[side, at]) * (w.dprob[side, at] - level))
            dv = [dot(e_ref[side], grad, down) for side in range(2)]
            w.wide_b[m, :, lanes(2)] = low(jnp.where(early, dv[0], dv[1]))
            dk = [dot(w.ds[side], queries, down) for side in range(2)]
            w.wide_b[m, :, lanes(1)] = low(jnp.where(early, dk[0], dk[1]))
            dq = [dot(w.ds[side], keys) for side in range(2)]
            w.wide_b[m, :, lanes(0)] = low(SCALE * jnp.where(early, dq[0], dq[1]))
            ticks(spread)
            if between is not None and pair == 0:
                between()
        if m == 0:
            got("joint")
        if s == 0:
            dn[1][m].wait_send()
        for r in (0, rows):
            at = pl.ds(r, rows)
            dq, dk, dv = (w.wide_b[m, at, pl.ds(i * part, part)] for i in range(3))
            far = dot(dk, w.joint[1], across) + dot(dv, w.joint[2], across)
            near = dot(dq, w.joint[0], across)
            if s:
                w.dm_mine[m, at] = low(far)
                w.middle[m, at] = near + jnp.where(core == 0, far, 0.0)
            else:
                w.dn_mine[m, at] = low(near + far)
        if s:
            pl.when(core == 1)(lambda: far_copy(m).start())
        else:
            dn[0][m].start()

    def join(m):
        pl.when(core == 0)(lambda: far_copy(m).wait_recv())
        for at in row_blocks(every, 32):
            there = jnp.where(core == 0, wide(w.crossed[m, at]), 0.0)
            w.dn_mine[m, at] = low(w.middle[m, at] + there)
        dn[1][m].start()

    def attention_weights(s, spread):
        for m in range(packs):
            got(("normed", m))
            if s:
                got(("source", m))
        normed = [w.narrow.at[m] for m in range(packs)]
        source = [w.source.at[m] for m in range(packs)] if s else normed
        dq, dk, dv = (
            [w.wide_b.at[m, :, pl.ds(i * part, part)] for m in range(packs)] for i in range(3)
        )
        context = [w.wide_a.at[m, :, pl.ds(3 * part, part)] for m in range(packs)]
        da = [w.da.at[m] for m in range(packs)]
        number = 2 * inner // block
        for first in range(0, width, block):
            at = pl.ds(first, block)
            query = product([n.at[:, at] for n in normed], dq)
            key = product([n.at[:, at] for n in source], dk)

            def both(slot):
                put(slot, query, 0, pl.ds(0, part))
                put(slot, key, 0, pl.ds(part, part))

            emit(s, number, both)
            number += 1
            ticks(spread)
        size = 128
        per = block // size
        strips = [("value", r) for r in range(0, part, size)] + [("out", r) for r in range(0, part, size)]
        for first in range(0, len(strips), per):
            group = strips[first : first + per]

            def fill(slot):
                for i, (kind, r) in enumerate(group):
                    if kind == "value":
                        for side in range(width // part):
                            at = pl.ds(side * part + r, size)
                            value = product([n.at[:, at] for n in source], dv)
                            put(slot, value, i * size, pl.ds(side * part, part))
                    else:
                        value = product([c.at[:, pl.ds(r, size)] for c in context], da)
                        put(slot, value, i * size)

            emit(s, number, fill)
            number += 1
            ticks(spread)
        settle_stores()
        ready[0] = (0 if s else count) + 2 * number

    def leave(s, m):
        dn[s][m].wait_recv()
        got(("base", m))
        totals = [0.0, 0.0]
        for r in range(0, every if s else rows, 32):
            peer, mine = pl.ds(r, 32), pl.ds(r if s else pl.multiple_of(own + r, 32), 32)
            grad = wide(w.dn_mine[m, mine]) + wide(w.dn_peer[m, peer])
            pulled, along = norm_rows_back(wide(w.base[m, peer]), grad, small[s, pl.ds(0, 1)])
            result = low(w.dmid[m, mine] + pulled)
            if s:
                w.dy[m, peer] = result
            else:
                w.dx[m, peer] = result
            for i, piece in enumerate((along, grad)):
                totals[i] = totals[i] + column_sum(piece)
        scale = 0.5 if s else 1.0
        add_sums(s, m, 0, scale * totals[0])
        add_sums(s, m, 2, scale * totals[1])

    def vectors(s):
        return remote(w.sums.at[s], w.sums_peer.at[s], w.v_send.at[s], w.v_recv.at[s], x_peer)

    def tail_store(s):
        return pltpu.make_async_copy(w.tail, g_refs[s].at[count - 1], w.t_store.at[s])

    def finish_vectors(s):
        vectors(s).wait()
        row = lax.broadcasted_iota(jnp.int32, (8, 1), 0)
        total = w.sums[s] + jnp.where(row < VECTORS, w.sums_peer[s], 0.0)
        if s:
            w.tail[...] = jnp.zeros(w.tail.shape, w.tail.dtype)
        pad = jnp.zeros((w.tail.shape[1] - 8, width), jnp.float32)
        w.tail[0] = low(jnp.concatenate([total, pad]))
        tail_store(s).start()
        tail_store(s).wait()
        ready[0] = count if s else 2 * count

    def ends_copy(m):
        return remote(
            y_in.at[m, pl.ds(theirs, rows)], w.ends_peer.at[m], w.y_send.at[m], w.y_recv.at[m], x_peer
        )

    def ends(m):
        ends_copy(m).wait()
        for at in row_blocks(rows, 32):
            w.ends_mine[m, at] = low(w.ends[m, at] + wide(w.ends_peer[m, at]))

    def edges_keep(src, b):
        return pltpu.make_async_copy(src, edges_ref.at[b], w.o_keep.at[0])

    def edges_hand(src, b):
        return remote(src, edges_ref.at[b], w.o_send.at[0], w.o_recv.at[0], sibling)

    def ask_base(s):
        for m in range(packs):
            if s:
                ask(("base", m), kept[s].base.at[m], w.base.at[m])
            else:
                ask(("base", m), kept[s].base.at[m, pl.ds(own, rows)], w.base.at[m, pl.ds(0, rows)])

    for s in (1, 0):
        if s:
            for m in range(packs):
                got(("dy", m))
        got("drop")
        got("lift")
        for m in range(packs):
            feed_forward(s, m)
            if not s:
                ticks(2)
        if not s:
            finish_vectors(1)
            for m in range(packs):
                ends(m)
            pl.when(core == 0)(lambda: edges_hand(w.ends_mine, 0).start())
            pl.when(core == 1)(lambda: edges_keep(w.ends_mine, 1).start())
        ask_base(s)
        if s:
            ask_layer(0)
            for m in range(packs):
                ends_copy(m).start()
        feed_forward_weights(s, 0 if s else 2)
        for m in range(packs):
            attention(s, m, 2, partial(join, m - 1) if s and m else None)
        if s:
            join(packs - 1)
        if s:
            ask_attention(0)
        attention_weights(s, 1)
        if s:
            ask_rows(0)
        for m in range(packs):
            leave(s, m)
            if s:
                ticks(2)
        vectors(s).start()
    finish_vectors(0)
    pl.when(core == 0)(lambda: edges_keep(w.dx, 0).start())
    pl.when(core == 1)(lambda: edges_hand(w.dx, 1).start())
    if inside:
        run_ticks(clock[0], length)
        drain()
    for m in range(packs):
        dn[0][m].wait_send()
    edges_keep(w.dx, 0).wait()
    edges_hand(w.dx, 0).wait()


def backward(line, small, dy, ends, weights, kept, inside):
    packs, every, width = dy.shape
    rows = every // 2
    inner, part = weights[0][0].shape[0], weights[0][3].shape[0]
    block = 8 * CHUNK
    count = (2 * inner + 4 * part) // (4 * CHUNK) + 1
    chunks = shape((count, 4, CHUNK, width))
    args = [small, dy, ends] + [a for s in range(2) for a in weights[s]] + [a for s in range(2) for a in kept[s]]
    anywhere = pl.BlockSpec(memory_space=pl.ANY)
    outs = [shape((2, packs, rows, width)), chunks, chunks]
    if inside:
        outs.append(shape((2,) + chunks.shape))
    names, scratch = backward_scratch(packs, rows, width, part, inner, block)
    if inside:
        bufs, sems = reducer_scratch(line, CHUNK, width)
        scratch = scratch + bufs + sems
    return pl.pallas_call(
        partial(backward_kernel, line, count, packs, inside, names),
        out_shape=outs,
        in_specs=[pl.BlockSpec(memory_space=pltpu.VMEM)] + [anywhere] * (len(args) - 1),
        out_specs=[anywhere] * len(outs),
        scratch_shapes=scratch,
        compiler_params=pltpu.CompilerParams(
            collective_id=2, has_side_effects=True, vmem_limit_bytes=62 * 1024 * 1024
        ),
    )(*args)


def local(
    edges_in,
    joint_weight,
    output_weight,
    lift_weight,
    lift_bias,
    drop_weight,
    norm_gains,
    norm_shifts,
    branch_biases,
    item_lengths,
    key_keep,
):
    half = lax.axis_index("tensor")
    held = edges_in[0]
    packs, _, width = held.shape[1:]
    part = joint_weight.shape[-1]
    inner = lift_weight.shape[-1]
    heads = part // HEAD_DIM
    head_ids = wide(half * heads + jnp.arange(heads, dtype=jnp.int32))
    slopes = jnp.power(2.0, -8.0 * (head_ids + 1.0) / HEADS)

    small = jnp.concatenate(
        [norm_gains[0], norm_shifts[0], branch_biases[0], lift_bias[0].reshape(2, -1, width)], axis=1
    )
    small = jnp.concatenate([small, jnp.zeros((2, 16 - small.shape[1], width), small.dtype)], axis=1)
    distances = jnp.stack(
        [masked_distance(item_lengths[0, m], key_keep[0, m]) for m in range(packs)]
    )
    given = (joint_weight[0], output_weight[0], small, lift_weight[0], drop_weight[0])
    kept, weights, small, dy, ends = forward(slopes, held, distances, given)
    line = lax.axis_size("dp") // 2
    inside = line == 4
    edges_out, *grads = backward(line, small, dy, ends, weights, kept, inside)
    grads = grads[2] if inside else reduce_over_dp(grads, line)
    grads = grads.reshape(2, -1, width)
    weight_rows = 2 * inner + 4 * part
    drop_grad, lift_grad, joint_grad, output_grad = widened(grads, inner, part)
    vectors = wide(grads[:, weight_rows : weight_rows + 6])
    lift_total = wide(grads[:, weight_rows + 6 : weight_rows + 6 + inner // width]).reshape(2, inner)
    return (
        edges_out[None],
        joint_grad[None],
        output_grad[None],
        lift_grad[None],
        lift_total[None],
        drop_grad[None],
        vectors[None, :, 0:2],
        vectors[None, :, 2:4],
        vectors[None, :, 4:6],
    )


def solution(mesh):
    in_specs = (
        P("section", None, None, ("dp", "tensor"), None),
        P("section", None, None, None, "tensor"),
        P("section", None, "tensor", None),
        P("section", None, None, "tensor"),
        P("section", None, "tensor"),
        P("section", None, "tensor", None),
        P("section", None, None, None),
        P("section", None, None, None),
        P("section", None, None, None),
        P("dp", None, None),
        P("dp", None, None),
    )
    out_specs = (
        P("section", None, None, ("dp", "tensor"), None),
        P("section", None, None, None, "tensor"),
        P("section", None, "tensor", None),
        P("section", None, None, "tensor"),
        P("section", None, "tensor"),
        P("section", None, "tensor", None),
        P("section", None, None, None),
        P("section", None, None, None),
        P("section", None, None, None),
    )
    return jax.shard_map(local, mesh=mesh, in_specs=in_specs, out_specs=out_specs, check_vma=False)
```

```python
from functools import partial

import jax
import jax.numpy as jnp
from jax import lax
from jax.experimental import pallas as pl
from jax.experimental.pallas import tpu as pltpu
from jax.sharding import PartitionSpec as P

HEADS = 12
HEAD_DIM = 64
EPSILON = 1e-06
SCALE = HEAD_DIM ** (-0.5)
FAR = 1e30
CHUNK = 32
AHEAD = 3
HOP = 2
VMEM_LIMIT = 44 * 1024 * 1024
MESH = pl.DeviceIdType.MESH


def swap(value, axis):
    return lax.ppermute(value, axis, [(0, 1), (1, 0)])


def pick(stacked, index, axis=0):
    return lax.dynamic_index_in_dim(stacked, index, axis, keepdims=False)


def masked_distance(lengths, keep_row):
    rows_all = keep_row.shape[0]
    slots = lengths.shape[0]
    positions = jnp.arange(rows_all, dtype=jnp.int32)
    ends = jnp.cumsum(lengths)
    segment = jnp.sum((positions[:, None] >= ends[None, :]).astype(jnp.int32), axis=1)
    following = jnp.arange(1, slots + 1, dtype=jnp.int32)
    item_ids = jnp.arange(slots, dtype=jnp.int32)
    begin = jnp.sum(jnp.where(segment[:, None] == following[None, :], ends[None, :], 0), axis=1)
    length = jnp.sum(jnp.where(segment[:, None] == item_ids[None, :], lengths[None, :], 0), axis=1)
    side = jnp.where(length == 144, 12, jnp.where(length == 225, 15, 20)).astype(jnp.int32)
    offset = positions - begin
    grid_row = (offset // side).astype(jnp.float32)
    column = (offset % side).astype(jnp.float32)
    row_gap = grid_row[:, None] - grid_row[None, :]
    col_gap = column[:, None] - column[None, :]
    distance = jnp.sqrt(row_gap * row_gap + col_gap * col_gap)
    allowed = (segment[:, None] == segment[None, :]) & (
        (keep_row[None, :] == 1) | (positions[:, None] == positions[None, :])
    )
    return jnp.where(allowed, distance, FAR)


def dot(a, b, dims=((1,), (0,))):
    return lax.dot_general(a, b, (dims, ((), ())), preferred_element_type=jnp.float32)


def low(value):
    return value.astype(jnp.bfloat16)


def wide(value):
    return value.astype(jnp.float32)


def shape(dims, dtype=jnp.bfloat16):
    return jax.ShapeDtypeStruct(tuple(dims), dtype)


def row_blocks(count, size=64):
    return [pl.ds(r, size) for r in range(0, count, size)]


def norm_rows(values, gain, shift):
    mean = jnp.mean(values, axis=-1, keepdims=True)
    centred = values - mean
    variance = jnp.mean(centred * centred, axis=-1, keepdims=True)
    return centred * lax.rsqrt(variance + EPSILON) * gain + shift


def norm_rows_back(values, grad, gain):
    mean = jnp.mean(values, axis=-1, keepdims=True)
    centred = values - mean
    variance = jnp.mean(centred * centred, axis=-1, keepdims=True)
    spread = lax.rsqrt(variance + EPSILON)
    unit = centred * spread
    scaled = grad * gain
    along = jnp.mean(scaled * unit, axis=-1, keepdims=True)
    level = jnp.mean(scaled, axis=-1, keepdims=True)
    return spread * (scaled - level - unit * along), grad * unit


def column_sum(value):
    return jnp.sum(value, axis=0, keepdims=True)


def widen_kernel(each, g_ref, drop, lift, joint, out, held, square, triple, last, load_sem, store_sem):
    streams, _, width = g_ref.shape
    part = out.shape[1]
    blocks = 2 * each + 2

    def load(b, i):
        return pltpu.make_async_copy(
            g_ref.at[b, pl.ds(i * width, width)], held.at[b, i], load_sem.at[b, i]
        )

    def store(b, i):
        if i < each:
            src, dst = square.at[b, i], drop.at[b, pl.ds(i * width, width)]
        elif i < 2 * each:
            src, dst = square.at[b, i], lift.at[b, :, pl.ds((i - each) * width, width)]
        elif i == 2 * each:
            src, dst = triple.at[b, pl.ds(0, 2)], joint.at[b, pl.ds(0, 2)]
        else:
            src, dst = triple.at[b, 2], joint.at[b, 2]
        return pltpu.make_async_copy(src, dst, store_sem.at[b, i])

    def store_out(b):
        return pltpu.make_async_copy(last.at[b], out.at[b], store_sem.at[b, blocks])

    every = [(b, i) for i in range(blocks) for b in range(streams)]
    for b, i in every:
        load(b, i).start()
    size = 64
    for b, i in every:
        load(b, i).wait()
        if i < 2 * each:

            @pl.loop(0, width // size)
            def _(r):
                at = pl.ds(pl.multiple_of(r * size, size), size)
                square[b, i, at] = wide(held[b, i, at])

        elif i == 2 * each:

            @pl.loop(0, width // size)
            def _(r):
                at = pl.ds(pl.multiple_of(r * size, size), size)
                for n in range(2):
                    triple[b, n, at] = wide(held[b, i, at, pl.ds(n * part, part)])

        else:

            @pl.loop(0, part // size)
            def _(r):
                at = pl.ds(pl.multiple_of(r * size, size), size)
                low_at = pl.ds(pl.multiple_of(part + r * size, size), size)
                triple[b, 2, at] = wide(held[b, i, at, pl.ds(0, part)])
                triple[b, 2, low_at] = wide(held[b, i, at, pl.ds(part, part)])
                last[b, at] = wide(held[b, i, low_at])

            store_out(b).start()
        store(b, i).start()
    for b, i in every:
        store(b, i).wait()
    for b in range(streams):
        store_out(b).wait()


def widened(grads, inner, part):
    streams, _, width = grads.shape
    each = inner // width
    f32 = jnp.float32
    outs = [(streams, inner, width), (streams, width, inner), (streams, 3, width, part), (streams, part, width)]
    anywhere = pl.BlockSpec(memory_space=pl.ANY)
    return pl.pallas_call(
        partial(widen_kernel, each),
        in_specs=[anywhere],
        out_specs=[anywhere] * 4,
        out_shape=[shape(dims, f32) for dims in outs],
        scratch_shapes=[
            pltpu.VMEM((streams, 2 * each + 2, width, width), jnp.bfloat16),
            pltpu.VMEM((streams, 2 * each, width, width), f32),
            pltpu.VMEM(outs[2], f32),
            pltpu.VMEM(outs[3], f32),
            pltpu.SemaphoreType.DMA((streams, 2 * each + 2)),
            pltpu.SemaphoreType.DMA((streams, 2 * each + 3)),
        ],
        compiler_params=pltpu.CompilerParams(vmem_limit_bytes=52 * 1024 * 1024),
    )(grads)


class Names:
    def __init__(self, pairs):
        for name, ref in pairs:
            setattr(self, name, ref)


KEPT = tuple(dict(qkvc=0, e=0, inv=0, normed=0, source=0, middle=0, mixed=0, act=0, steep=0, base=0))
WEIGHTS = tuple(dict(drop=0, lift=0, joint=0, out=0))
GIVEN = tuple(dict(joint=0, out=0, small=0, lift=0, drop=0))
VECTORS = 6
LOADS = 64


def kept_shapes(s, packs, every, width, part, inner):
    heads = part // HEAD_DIM
    f32 = jnp.float32
    dims = dict(
        qkvc=shape((packs, every, 4 * part)),
        e=shape((packs, heads, every, every)),
        inv=shape((packs, every, part), f32),
        normed=shape((packs, every, width)),
        source=shape((packs, every, width)),
        middle=shape((packs, every, width), f32),
        mixed=shape((packs, every, width)),
        act=shape((packs, every, inner)),
        steep=shape((packs, every, inner)),
        base=shape((packs, every, width)),
    )
    if s == 0:
        dims.pop("source")
    return dims


def forward_plan(packs, every, width, part, inner):
    full, f32, bf16 = (packs, every, width), jnp.float32, jnp.bfloat16
    rooms = dict(
        joint=((2, 3, width, part), bf16),
        out=((2, part, width), bf16),
        small_in=((2, 16, width), bf16),
        lift=((2, width, inner), bf16),
        drop=((2, inner, width), bf16),
        dist=((packs, every, every), f32),
        rows_in=(full, bf16),
        base=(full, bf16),
        dy=(full, bf16),
        normed=(full, bf16),
        crossed=(full, bf16),
        source=(full, bf16),
        qkvc=((packs, every, 4 * part), bf16),
        e=((part // HEAD_DIM, every, every), bf16),
        inv=((packs, every, part), f32),
        a_mine=(full, bf16),
        a_peer=(full, bf16),
        y_mine=(full, bf16),
        y_peer=(full, bf16),
        middle=(full, f32),
        mixed=(full, bf16),
        act=((packs, every, inner), bf16),
        steep=((packs, every, inner), bf16),
        scores=((2, every, every), f32),
        hidden=((2, every, 256), f32),
    )
    sem = pltpu.SemaphoreType.DMA
    flags = dict(
        w_load=sem((5,)),
        w_send=sem((5,)),
        w_recv=sem((5,)),
        d_load=sem((packs,)),
        r_load=sem((2, packs)),
        r_send=sem((2, 2, 2, packs)),
        r_recv=sem((2, 2, packs)),
        x_send=sem((2, 2, packs)),
        x_recv=sem((2, 2, packs)),
        c_send=sem((packs,)),
        c_recv=sem((packs,)),
        store=sem((LOADS,)),
    )
    scratch = [pltpu.VMEM(*spec) for spec in rooms.values()] + list(flags.values())
    return list(rooms) + list(flags), scratch


def forward_kernel(packs, names, *refs):
    refs = list(refs)

    def take(n):
        taken = refs[:n]
        del refs[:n]
        return taken

    slopes, rows_ref = take(2)
    dist_refs = take(packs)
    given = dict(zip(GIVEN, take(5)))
    kept = [
        Names(zip([k for k in KEPT if s or k != "source"], take(len(KEPT) - (s == 0)))) for s in range(2)
    ]
    placed = [Names(zip(WEIGHTS, take(4))) for _ in range(2)]
    small_ref, dy_ref, y_ref = take(3)
    w = Names(zip(names, refs))
    core, half = lax.axis_index("section"), lax.axis_index("tensor")
    away = 1 - half
    every, width = w.base.shape[1:]
    rows = every // 2
    part, inner = w.out.shape[1], w.drop.shape[1]
    own = pl.ds(pl.multiple_of(half * rows, rows), rows)
    x_peer = {"tensor": away}
    sibling = {"section": 1 - core}
    early = lax.broadcasted_iota(jnp.int32, (1, 2 * HEAD_DIM), 1) < HEAD_DIM
    across = ((1,), (1,))

    def remote(src, dst, sent, got, target):
        return pltpu.make_async_remote_copy(
            src_ref=src, dst_ref=dst, send_sem=sent, recv_sem=got,
            device_id=target, device_id_type=MESH,
        )

    def weight_load(i):
        return pltpu.make_async_copy(
            given[GIVEN[i]].at[core], getattr(w, room[i]).at[core], w.w_load.at[i]
        )

    def weight_out(i):
        return remote(
            given[GIVEN[i]].at[1 - core], getattr(w, room[i]).at[core], w.w_send.at[i], w.w_recv.at[i], sibling
        )

    def dist_load(m):
        return pltpu.make_async_copy(dist_refs[m], w.dist.at[m], w.d_load.at[m])

    room = tuple("small_in" if name == "small" else name for name in GIVEN)
    lands = (w.rows_in, w.dy)

    def rows_load(kind, m):
        return pltpu.make_async_copy(rows_ref.at[kind, m], lands[kind].at[m, own], w.r_load.at[kind, m])

    def rows_out(kind, b, t, m):
        side = jnp.where(t == half, 0, 1)
        return remote(
            rows_ref.at[b, m], lands[kind].at[m, own], w.r_send.at[kind, b, side, m], w.r_recv.at[kind, side, m],
            {"section": b, "tensor": t},
        )

    def rows_start(kind, m):
        @pl.when(core == kind)
        def _():
            rows_out(kind, 1 - kind, away, m).start()
            rows_out(kind, kind, away, m).start()
            rows_out(kind, 1 - kind, half, m).start()

    def rows_got(kind, m):
        rows_out(kind, 0, away, m).wait_recv()

        @pl.when(core == kind)
        def _():
            rows_load(kind, m).wait()

        @pl.when(core != kind)
        def _():
            rows_out(kind, 0, half, m).wait_recv()

    def rows_sent(kind, m):
        @pl.when(core == kind)
        def _():
            rows_out(kind, 1 - kind, away, m).wait_send()
            rows_out(kind, kind, away, m).wait_send()
            rows_out(kind, 1 - kind, half, m).wait_send()

    for i in range(len(room)):
        weight_load(i).start()
    for m in range(packs):
        dist_load(m).start()
        for kind in range(2):
            pl.when(core == kind)(lambda: rows_load(kind, m).start())
    barrier = pltpu.get_barrier_semaphore()
    for c, t in [(1 - core, half), (core, away), (1 - core, away)]:
        pl.semaphore_signal(
            barrier, inc=1, device_id={"section": c, "tensor": t}, device_id_type=MESH
        )
    pl.semaphore_wait(barrier, 3)
    rows_start(0, 0)
    for i in range(3):
        weight_out(i).start()
    for m in range(1, packs):
        rows_start(0, m)
    for i in range(3, len(room)):
        weight_out(i).start()

    numbers = iter(range(LOADS))
    pending = {}

    def store(key, src, dst):
        copy = pltpu.make_async_copy(src, dst, w.store.at[next(numbers)])
        copy.start()
        pending[key] = copy

    def free(*key):
        if key in pending:
            pending.pop(key).wait()

    def keep(name, s, m):
        store((name, m), getattr(w, name).at[m], getattr(kept[s], name).at[m])

    def weight_got(name, s):
        i = room.index(name)
        pl.when(core == s)(lambda: weight_load(i).wait())
        pl.when(core != s)(lambda: weight_out(i).wait_recv())
        if name in WEIGHTS:
            store((name, "placed", s), getattr(w, name).at[s], getattr(placed[s], name))

    vectors = [None, None]

    def small_got(s):
        weight_got("small_in", s)
        vectors[s] = wide(w.small_in[s])
        small_ref[s] = vectors[s]

    def row(s, i):
        return vectors[s][i : i + 1]

    def over_x(src, dst, kind, s, m):
        return remote(src, dst, w.x_send.at[kind, s, m], w.x_recv.at[kind, s, m], x_peer)

    def a_copy(s, m):
        return over_x(w.a_mine.at[m], w.a_peer.at[m], 0, s, m)

    def y_copy(m):
        return over_x(w.y_mine.at[m], w.y_peer.at[m], 1, 0, m)

    def crossing(m):
        return remote(w.normed.at[m], w.crossed.at[m], w.c_send.at[m], w.c_recv.at[m], sibling)

    def attention(s, m):
        source = w.source if s else w.normed
        free("qkvc", m)
        w.qkvc[m, :, pl.ds(0, part)] = low(SCALE * dot(w.normed[m], w.joint[s, 0]))
        if s:

            @pl.when(core == 0)
            def _():
                w.source[m] = w.normed[m]

            @pl.when(core == 1)
            def _():
                crossing(m).wait_recv()
                w.source[m] = w.crossed[m]

            keep("source", s, m)
        for i in (1, 2):
            w.qkvc[m, :, pl.ds(i * part, part)] = low(dot(source[m], w.joint[s, i]))
        if s == 0:
            dist_load(m).wait()
        free("inv", m)
        free("e")

        @pl.loop(0, part // (2 * HEAD_DIM))
        def _(pair):
            def lanes(i):
                start = i * part + pair * 2 * HEAD_DIM
                return pl.ds(pl.multiple_of(start, 2 * HEAD_DIM), 2 * HEAD_DIM)

            queries, keys, values = (w.qkvc[m, :, lanes(i)] for i in range(3))
            for side in range(2):
                here = early if side == 0 else jnp.logical_not(early)
                w.scores[side] = dot(jnp.where(here, queries, 0), keys, across)
            for side in range(2):
                head = 2 * pair + side
                here = early if side == 0 else jnp.logical_not(early)
                slope = slopes[head]
                for at in row_blocks(every):
                    value = w.scores[side, at] - slope * w.dist[m, at]
                    expo = jnp.exp(value - jnp.max(value, axis=-1, keepdims=True))
                    w.e[head, at] = low(expo)
                    inverse = 1.0 / jnp.sum(expo, axis=-1, keepdims=True)
                    if side == 0:
                        w.inv[m, at, lanes(0)] = jnp.broadcast_to(inverse, (64, 2 * HEAD_DIM))
                    else:
                        w.inv[m, at, lanes(0)] = jnp.where(here, inverse, w.inv[m, at, lanes(0)])
            sums = [dot(w.e[2 * pair + side], values) for side in range(2)]
            context = jnp.where(early, sums[0], sums[1]) * w.inv[m, :, lanes(0)]
            w.qkvc[m, :, lanes(3)] = low(context)

        if m == 0:
            weight_got("out", s)
        if s:
            a_copy(0, m).wait_send()
        for r in (0, rows):
            at = pl.ds(r, rows)
            w.a_mine[m, at] = low(dot(w.qkvc[m, at, pl.ds(3 * part, part)], w.out[s]))
        a_copy(s, m).start()
        store(("e",), w.e, kept[s].e.at[m])
        keep("qkvc", s, m)
        keep("inv", s, m)

    def feed_forward(s, m):
        base = w.base if s else w.rows_in
        a_copy(s, m).wait_recv()
        for name in ("middle", "mixed", "act", "steep"):
            free(name, m)
        for at in row_blocks(every):
            total = wide(w.a_mine[m, at]) + wide(w.a_peer[m, at])
            value = wide(base[m, at]) + total + row(s, 4)
            w.middle[m, at] = value
            w.mixed[m, at] = low(norm_rows(value, row(s, 1), row(s, 3)))
        if m == 0:
            weight_got("lift", s)
            weight_got("drop", s)
        size = w.hidden.shape[-1]
        for number in range(inner // size):
            lanes = pl.ds(number * size, size)
            at, off = divmod(number * size, width)
            bias = vectors[s][VECTORS + at : VECTORS + at + 1, off : off + size]
            w.hidden[number % 2] = dot(w.mixed[m], w.lift[s, :, lanes])
            for at in row_blocks(every):
                value = w.hidden[number % 2, at] + bias
                below = 0.5 + 0.5 * lax.erf(value * (0.5**0.5))
                density = 0.3989422804014327 * jnp.exp(-0.5 * value * value)
                w.act[m, at, lanes] = low(value * below)
                w.steep[m, at, lanes] = low(below + value * density)
        if s:
            y_copy(m).wait_send()
        for r in (0, rows):
            at = pl.ds(r, rows)
            w.y_mine[m, at] = low(dot(w.act[m, at], w.drop[s]))
        if s == 0:
            y_copy(m).start()
        else:
            store(("y", m), w.y_mine.at[m], y_ref.at[m])
        for name in ("middle", "mixed", "act", "steep"):
            keep(name, s, m)

    def enter(m):
        y_copy(m).wait_recv()
        free("normed", m)
        for at in row_blocks(every):
            total = wide(w.y_mine[m, at]) + wide(w.y_peer[m, at])
            value = low(w.middle[m, at] + total + row(0, 5))
            w.base[m, at] = value
            w.normed[m, at] = low(norm_rows(wide(value), row(1, 0), row(1, 2)))
        pl.when(core == 0)(lambda: crossing(m).start())
        keep("base", 1, m)
        keep("normed", 1, m)

    small_got(0)
    weight_got("joint", 0)
    for m in range(packs):
        rows_got(0, m)
        for at in row_blocks(every):
            w.normed[m, at] = low(norm_rows(wide(w.rows_in[m, at]), row(0, 0), row(0, 2)))
        store(("rows", m), w.rows_in.at[m], kept[0].base.at[m])
        keep("normed", 0, m)
        attention(0, m)
    for m in range(packs):
        feed_forward(0, m)
    small_got(1)
    weight_got("joint", 1)
    for m in range(packs):
        enter(m)
        attention(1, m)
    for m in range(packs):
        rows_start(1, m)
    for m in range(packs):
        feed_forward(1, m)
    for m in range(packs):
        rows_got(1, m)
        store(("dy", m), w.dy.at[m], dy_ref.at[m])
    for i in range(len(room)):
        weight_out(i).wait_send()
    for m in range(packs):
        for kind in range(2):
            rows_sent(kind, m)
        a_copy(1, m).wait_send()
        pl.when(core == 0)(lambda: crossing(m).wait_send())
    for key in list(pending):
        free(*key)


def forward(slopes, held, distances, weights):
    packs, rows, width = held.shape[1:]
    every = 2 * rows
    part, inner = weights[1].shape[1], weights[4].shape[1]
    order = dict(zip(GIVEN, weights))
    kept = [kept_shapes(s, packs, every, width, part, inner) for s in range(2)]
    outs = list(kept[0].values()) + list(kept[1].values())
    outs += [shape(order[name].shape[1:]) for name in WEIGHTS] * 2
    outs += [shape((2, 16, width), jnp.float32), shape((packs, every, width)), shape((packs, every, width))]
    names, scratch = forward_plan(packs, every, width, part, inner)
    anywhere = pl.BlockSpec(memory_space=pl.ANY)
    out_specs = [anywhere] * len(outs)
    out_specs[-3] = pl.BlockSpec(memory_space=pltpu.VMEM)
    found = list(
        pl.pallas_call(
            partial(forward_kernel, packs, names),
            out_shape=outs,
            in_specs=[pl.BlockSpec(memory_space=pltpu.SMEM)] + [anywhere] * (6 + packs),
            out_specs=out_specs,
            scratch_shapes=scratch,
            compiler_params=pltpu.CompilerParams(
                collective_id=1, has_side_effects=True, vmem_limit_bytes=60 * 1024 * 1024
            ),
        )(slopes, held, *distances, *weights)
    )
    results = []
    for s in range(2):
        layer = {name: found.pop(0) for name in kept[s]}
        layer.setdefault("source", layer["normed"])
        results.append([layer[name] for name in KEPT])
    placed = [[found.pop(0) for _ in WEIGHTS] for _ in range(2)]
    return results, placed, *found


def reducer(line, count, g_refs, o_ref, bufs, sems):
    load_ring, loads_ring, from_y, from_prv, from_nxt, both, mid2, from_y2, res2 = bufs
    load_sem, y_send, y_recv, n_send, n_recv, p_send, p_recv, f_send = sems[:8]
    load2, n2_send, p2_recv, m2_recv, u2_send, u2_recv, a2_send, r2_recv, o2_send = sems[8:17]
    s_send, l_sem, s2_send, l2_sem, f_recv, d_recv, s_recv = sems[17:]
    dp = lax.axis_index("dp")
    core = lax.axis_index("section")
    y, z = dp % 2, dp // 2
    depth = line // 2 - 1
    left = z < line // 2
    step = jnp.where(left, 1, -1)
    edge = jnp.where(left, z, line - 1 - z)
    mine = jnp.where(left, 0, 1)
    total = 2 * count
    slots = from_y.shape[0]
    ring = load_ring.shape[0]
    inner = edge == depth
    outer = jnp.logical_not(inner)

    def device(z_at, y_at, core_at):
        return {"dp": z_at * 2 + y_at, "section": core_at}

    across = device(z, 1 - y, core)
    across_other = device(z, 1 - y, 1 - core)
    sibling = device(z, y, 1 - core)
    nxt = device(z + step, y, core)
    prv = device(z - step, y, core)

    def greet(extra):
        barrier = pltpu.get_barrier_semaphore()
        targets = [across, across_other, sibling, nxt] + extra
        for target in targets:
            pl.semaphore_signal(barrier, inc=1, device_id=target, device_id_type=MESH)

        @pl.when(edge > 0)
        def _():
            pl.semaphore_signal(barrier, inc=1, device_id=prv, device_id_type=MESH)

        pl.semaphore_wait(barrier, len(targets) + jnp.where(edge > 0, 1, 0))

    def send(src, dst, sent, got, target):
        return pltpu.make_async_remote_copy(
            src_ref=src,
            dst_ref=dst,
            send_sem=sent,
            recv_sem=got,
            device_id=target,
            device_id_type=MESH,
        )

    def plus(into, other):
        return (into.astype(jnp.float32) + other.astype(jnp.float32)).astype(into.dtype)

    def guarded(k, body):
        pl.when((k >= 0) & (k < total))(lambda: body(k))

    def by_layer(k, body):
        pl.when(k < count)(lambda: body(g_refs[1], k))
        pl.when(k >= count)(lambda: body(g_refs[0], k - count))

    def stays(k):
        return jnp.where(k < count, 1, 0) == core

    def place(k):
        return jnp.where(k < count, k, k - count)

    def load(k, g_ref=g_refs[0], j=0):
        return pltpu.make_async_copy(g_ref.at[j, y], load_ring.at[k % ring], load_sem.at[k % ring])

    def over_y(k, g_ref=g_refs[0], j=0):
        i = k % slots
        return send(g_ref.at[j, 1 - y], from_y.at[i], y_send.at[i], y_recv.at[i], across)

    def inward(k):
        i = k % slots
        return send(from_y.at[i], from_prv.at[i], n_send.at[i], p_recv.at[i], nxt)

    def middle(k):
        i = k % slots
        return send(from_y.at[i], from_nxt.at[i], n_send.at[i], n_recv.at[i], nxt)

    def outward(k):
        i = k % slots
        return send(from_nxt.at[i], from_nxt.at[i], p_send.at[i], n_recv.at[i], prv)

    def keep(k):
        i = k % slots
        return pltpu.make_async_copy(from_nxt.at[i], o_ref.at[core, place(k), y], l_sem.at[i])

    def hand(k):
        i = k % slots
        return send(from_nxt.at[i], o_ref.at[core, place(k), y], s_send.at[i], s_recv, sibling)

    def back_same(k):
        i = k % slots
        return send(from_nxt.at[i], o_ref.at[core, place(k), y], f_send.at[i], f_recv, across)

    def back_other(k):
        i = k % slots
        return send(from_nxt.at[i], o_ref.at[core, place(k), y], f_send.at[i], d_recv, across_other)

    def begin(k):
        def one(g_ref, j):
            over_y(k, g_ref, j).start()
            load(k, g_ref, j).start()

        by_layer(k, one)

    def pair(k):
        load(k).wait()
        over_y(k).wait()
        i = k % slots
        from_y[i] = plus(from_y[i], load_ring[k % ring])

    def pass_on(k):
        i = k % slots

        @pl.when(edge > 0)
        def _():
            inward(k).wait_recv()
            from_y[i] = plus(from_y[i], from_prv[i])

        pl.when(inner)(lambda: middle(k).start())
        pl.when(outer)(lambda: inward(k).start())

    def finish(k):
        i = k % slots
        middle(k).wait()

        @pl.when(inner)
        def _():
            from_nxt[i] = plus(from_nxt[i], from_y[i])

        pl.when(edge > 0)(lambda: outward(k).start())

        @pl.when(stays(k))
        def _():
            back_same(k).start()
            keep(k).start()

        @pl.when(jnp.logical_not(stays(k)))
        def _():
            back_other(k).start()
            hand(k).start()

    def loads(k, g_ref=g_refs[0], j=0, into=None):
        into = loads_ring.at[k % ring] if into is None else into
        return pltpu.make_async_copy(g_ref.at[j, pl.ds(2, 2)], into, load2.at[k % ring])

    def inwards(k):
        i = k % slots
        return send(both.at[i], both.at[i], n2_send.at[i], p2_recv.at[i], nxt)

    def halve(k):
        i = k % slots
        return send(both.at[i, 1 - mine], mid2.at[i], n2_send.at[i], m2_recv.at[i], nxt)

    def trade(k):
        i = k % slots
        return send(both.at[i, mine], from_y2.at[i], u2_send.at[i], u2_recv.at[i], across)

    def rejoin(k, q):
        i = k % slots
        return send(res2.at[i, q], res2.at[i, q], a2_send.at[i], r2_recv.at[i, q], nxt)

    def outwards(k, q):
        i = k % slots
        return send(res2.at[i, q], res2.at[i, q], o2_send.at[i, q], r2_recv.at[i, q], prv)

    def keep2(k, q):
        i = k % slots
        return pltpu.make_async_copy(
            res2.at[i, q], o_ref.at[core, place(k), 2 + q], l2_sem.at[i, q]
        )

    def hand2(k, q):
        i = k % slots
        return send(res2.at[i, q], o_ref.at[core, place(k), 2 + q], s2_send.at[i, q], s_recv, sibling)

    def spread(k, q):
        pl.when(edge > 0)(lambda: outwards(k, q).start())
        pl.when(stays(k))(lambda: keep2(k, q).start())
        pl.when(jnp.logical_not(stays(k)))(lambda: hand2(k, q).start())

    def begin2(k):
        def one(g_ref, j):
            pl.when(edge == 0)(lambda: loads(k, g_ref, j, both.at[k % slots]).start())
            pl.when(edge > 0)(lambda: loads(k, g_ref, j).start())

        by_layer(k, one)

    def pass_on2(k):
        i = k % slots
        loads(k).wait()

        @pl.when(edge > 0)
        def _():
            inwards(k).wait_recv()
            both[i] = plus(both[i], loads_ring[k % ring])

        pl.when(inner)(lambda: halve(k).start())
        pl.when(outer)(lambda: inwards(k).start())

    def trade2(k):
        i = k % slots
        halve(k).wait()
        both[i, mine] = plus(both[i, mine], mid2[i])
        trade(k).start()

    def settle2(k):
        i = k % slots
        trade(k).wait()
        res2[i, mine] = plus(both[i, mine], from_y2[i])
        rejoin(k, mine).start()
        spread(k, mine)

    def finish2(k):
        @pl.when(inner)
        def _():
            rejoin(k, 1 - mine).wait_recv()
            spread(k, 1 - mine)

        @pl.when(outer)
        def _():
            inwards(k).wait_send()
            for q in range(2):
                rejoin(k, q).wait_recv()
                spread(k, q)

    def retire(k):
        @pl.when(inner)
        def _():
            rejoin(k, mine).wait_send()

        @pl.when(edge > 0)
        def _():
            outward(k).wait_send()
            for q in range(2):
                outwards(k, q).wait_send()

        back_same(k).wait_send()

        @pl.when(stays(k))
        def _():
            keep(k).wait()
            for q in range(2):
                keep2(k, q).wait()

        @pl.when(jnp.logical_not(stays(k)))
        def _():
            hand(k).wait_send()
            for q in range(2):
                hand2(k, q).wait_send()

    span = AHEAD + HOP * (2 * depth + 3) + 1

    def ticks(first, last):
        @pl.loop(first, last)
        def _(tick):
            now = tick - AHEAD
            guarded(tick - span, retire)
            guarded(tick, begin)
            guarded(now, pair)
            guarded(tick - HOP * edge, begin2)
            guarded(now - HOP * edge, pass_on)
            guarded(now - HOP * edge, pass_on2)

            @pl.when(inner)
            def _():
                guarded(now - HOP * (depth + 1), trade2)
                guarded(now - HOP * (depth + 2), settle2)

            guarded(now - HOP * (2 * depth + 1 - edge), finish)
            guarded(now - HOP * (2 * depth + 3 - edge), finish2)

    def drain():
        group = o_ref.at[0, :, 0]
        groups = o_ref.at[0, :, pl.ds(0, 3)]
        pltpu.make_async_copy(group, group, f_recv).wait()
        pltpu.make_async_copy(group, group, d_recv).wait()
        pltpu.make_async_copy(groups, groups, s_recv).wait()

    return greet, ticks, drain, total + span


def reducer_scratch(line, rows, width):
    slots = AHEAD + HOP * (line + 1) + 3
    ring = AHEAD + 1

    def room(*lead):
        return pltpu.VMEM(lead + (rows, width), jnp.bfloat16)

    def sems(*dims):
        return pltpu.SemaphoreType.DMA(dims)

    bufs = [room(ring), room(ring, 2)] + [room(slots)] * 3 + [room(slots, 2)]
    bufs += [room(slots)] * 2 + [room(slots, 2)]
    many, twice = sems(slots), sems(slots, 2)
    flags = [sems(ring)] + [many] * 7 + [sems(ring)] + [many] * 6 + [twice] * 2
    return bufs, flags + [many] * 2 + [twice] * 2 + [pltpu.SemaphoreType.DMA] * 3


BUFS, SEMS = 9, 24


def reduce_kernel(line, count, g_zero, g_one, o_ref, *refs):
    greet, ticks, drain, length = reducer(
        line, count, (g_zero, g_one), o_ref, refs[:BUFS], refs[BUFS:]
    )
    greet([])
    ticks(0, length)
    drain()


def reduce_over_dp(grads, line):
    count, _, rows, width = grads[0].shape
    bufs, sems = reducer_scratch(line, rows, width)
    return pl.pallas_call(
        partial(reduce_kernel, line, count),
        out_shape=shape((2,) + grads[0].shape),
        in_specs=[pl.BlockSpec(memory_space=pl.ANY)] * 2,
        out_specs=pl.BlockSpec(memory_space=pl.ANY),
        scratch_shapes=bufs + sems,
        compiler_params=pltpu.CompilerParams(
            collective_id=0, has_side_effects=True, vmem_limit_bytes=56 * 1024 * 1024
        ),
    )(*grads)


def backward_scratch(packs, rows, width, part, inner, block):
    full, f32 = (packs, 2 * rows, width), jnp.float32
    bf16 = jnp.bfloat16
    plan = dict(
        drop=((inner, width), bf16),
        lift=((width, inner), bf16),
        joint=((3, width, part), bf16),
        out=((part, width), bf16),
        dy=(full, bf16),
        wide_a=((packs, 2 * rows, inner), bf16),
        wide_b=((packs, 2 * rows, inner), bf16),
        narrow=(full, bf16),
        source=(full, bf16),
        dm_mine=(full, bf16),
        dm_peer=(full, bf16),
        dn_mine=(full, bf16),
        dn_peer=(full, bf16),
        crossed=(full, bf16),
        middle=(full, f32),
        dmid=(full, f32),
        da=(full, bf16),
        inv=((packs, 2 * rows, part), f32),
        base=(full, bf16),
        ends=((packs, rows, width), f32),
        ends_mine=((packs, rows, width), bf16),
        ends_peer=((packs, rows, width), bf16),
        dx=((packs, rows, width), bf16),
        e=((2, 2, 2 * rows, 2 * rows), bf16),
        dc=((2 * rows, part), f32),
        dprob=((2, 2 * rows, 2 * rows), f32),
        ds=((2, 2 * rows, 2 * rows), bf16),
        staged=((3, 2, 4, block // 8, width), bf16),
        sums=((2, 8, width), f32),
        sums_peer=((2, 8, width), f32),
        tail=((4, block // 8, width), bf16),
    )
    sem = pltpu.SemaphoreType.DMA
    flags = dict(
        load=sem((LOADS,)),
        e_load=sem((2,)),
        x_send=sem((2, 2, packs)),
        x_recv=sem((2, 2, packs)),
        c_send=sem((packs,)),
        c_recv=sem((packs,)),
        g_store=sem((3,)),
        t_store=sem((2,)),
        v_send=sem((2,)),
        v_recv=sem((2,)),
        y_send=sem((packs,)),
        y_recv=sem((packs,)),
        o_keep=sem((1,)),
        o_send=sem((1,)),
        o_recv=sem((1,)),
    )
    return list(plan) + list(flags), [pltpu.VMEM(*spec) for spec in plan.values()] + list(flags.values())


def backward_kernel(line, count, packs, inside, names, *refs):
    refs = list(refs)

    def take(n):
        taken = refs[:n]
        del refs[:n]
        return taken

    small, dy_in, y_in = take(3)
    weights = [Names(zip(WEIGHTS, take(4))) for _ in range(2)]
    kept = [Names(zip(KEPT, take(len(KEPT)))) for _ in range(2)]
    edges_ref, *g_refs = take(3)
    o_ref = take(1)[0] if inside else None
    w = Names(zip(names, take(len(names))))
    core, half = lax.axis_index("section"), lax.axis_index("tensor")
    every, width = w.dy.shape[1:]
    rows = every // 2
    part, inner = w.out.shape[0], w.drop.shape[0]
    block = 8 * w.tail.shape[1]
    pairs = part // (2 * HEAD_DIM)
    x_peer = {"tensor": 1 - half}
    sibling = {"section": 1 - core}
    own = pl.multiple_of(half * rows, rows)
    theirs = pl.multiple_of((1 - half) * rows, rows)
    early = lax.broadcasted_iota(jnp.int32, (1, 2 * HEAD_DIM), 1) < HEAD_DIM
    numbers = iter(range(LOADS))
    down, across = ((0,), (0,)), ((1,), (1,))

    def fetch(src, dst):
        copy = pltpu.make_async_copy(src, dst, w.load.at[next(numbers)])
        copy.start()
        return copy

    def remote(src, dst, sent, got, target):
        return pltpu.make_async_remote_copy(
            src_ref=src, dst_ref=dst, send_sem=sent, recv_sem=got,
            device_id=target, device_id_type=MESH,
        )

    def over_x(src, dst, kind, s, m):
        return remote(src, dst, w.x_send.at[kind, s, m], w.x_recv.at[kind, s, m], x_peer)

    pending = {}

    def ask(key, src, dst):
        pending[key] = fetch(src, dst)

    def got(key):
        pending.pop(key).wait()

    def ask_layer(s):
        for name in ("drop", "lift"):
            ask(name, getattr(weights[s], name), getattr(w, name))

    def ask_rows(s):
        for m in range(packs):
            ask(("act", m), kept[s].act.at[m], w.wide_a.at[m])
            ask(("steep", m), kept[s].steep.at[m], w.wide_b.at[m])
            ask(("mixed", m), kept[s].mixed.at[m], w.narrow.at[m])

    def ask_attention(s):
        for name in ("joint", "out"):
            ask(name, getattr(weights[s], name), getattr(w, name))
        for m in range(packs):
            ask(("middle", m), kept[s].middle.at[m], w.middle.at[m])
            ask(("inv", m), kept[s].inv.at[m], w.inv.at[m])

    for m in range(packs):
        ask(("dy", m), dy_in.at[m], w.dy.at[m])
        ask(("ends", m), y_in.at[m, pl.ds(own, rows)], w.ends_mine.at[m])
    ask_rows(1)
    ask_layer(1)
    ask_attention(1)

    clock, ready = [0], [0]
    if inside:
        greet, run_ticks, drain, length = reducer(
            line, count, g_refs, o_ref, refs[:BUFS], refs[BUFS:]
        )
        greet([x_peer])

        def ticks(n):
            n = min(n, ready[0] - clock[0])
            if n > 0:
                run_ticks(clock[0], clock[0] + n)
                clock[0] += n
    else:
        barrier = pltpu.get_barrier_semaphore()
        for target in (x_peer, sibling):
            pl.semaphore_signal(barrier, inc=1, device_id=target, device_id_type=MESH)
        pl.semaphore_wait(barrier, 2)

        def ticks(n):
            pass

    def add_sums(s, m, row, value):
        at = pl.ds(row, 1)
        w.sums[s, at] = value if m == 0 else w.sums[s, at] + value

    stores = [None, None, None]
    stored = [0]

    def emit(s, number, fill):
        slot = stored[0] % 3
        stored[0] += 1
        if stores[slot] is not None:
            stores[slot].wait()
        fill(slot)
        stores[slot] = pltpu.make_async_copy(
            w.staged.at[slot], g_refs[s].at[pl.ds(2 * number, 2)], w.g_store.at[slot]
        )
        stores[slot].start()

    def settle_stores():
        for slot in range(3):
            if stores[slot] is not None:
                stores[slot].wait()
                stores[slot] = None

    def put(slot, value, first=0, lanes=slice(None)):
        step = block // 8
        per = 4 * step
        for r in range(0, value.shape[0], step):
            at = first + r
            w.staged[slot, at // per, at % per // step, :, lanes] = low(value[r : r + step])

    def product(lefts, rights):
        return sum(dot(a[...], b[...], down) for a, b in zip(lefts, rights))

    dm = [[over_x(w.dm_mine.at[m], w.dm_peer.at[m], 0, s, m) for m in range(packs)] for s in range(2)]
    dn = [
        [
            over_x(
                w.dn_mine.at[m, pl.ds(theirs, rows)],
                w.dn_peer.at[m, pl.ds(0, rows)],
                1, 0, m,
            )
            for m in range(packs)
        ],
        [over_x(w.dn_mine.at[m], w.dn_peer.at[m], 1, 1, m) for m in range(packs)],
    ]

    def far_copy(m):
        return remote(w.dm_mine.at[m], w.crossed.at[m], w.c_send.at[m], w.c_recv.at[m], sibling)

    def feed_forward(s, m):
        got(("steep", m))
        if s == 0:
            pl.when(core == 1)(lambda: far_copy(m).wait_send())
        size = 256
        for number in range(inner // size):
            lanes = pl.ds(number * size, size)
            grad = dot(w.dy[m], w.drop[lanes], across) * wide(w.wide_b[m, :, lanes])
            grad = low(grad)
            w.wide_b[m, :, lanes] = grad
            total = column_sum(wide(grad))
            at = number * size
            spot = (s, pl.ds(VECTORS + at // width, 1), pl.ds(at % width, size))
            w.sums[spot] = total if m == 0 else w.sums[spot] + total
        add_sums(s, m, 5, 0.5 * column_sum(wide(w.dy[m])))
        for r in (0, rows):
            at = pl.ds(r, rows)
            w.dm_mine[m, at] = low(dot(w.wide_b[m, at], w.lift[...], across))
        dm[s][m].start()

    def drop_weights(s, spread):
        for m in range(packs):
            got(("act", m))
        for number, first in enumerate(range(0, inner, block)):
            lanes = pl.ds(first, block)
            value = product([w.wide_a.at[m, :, lanes] for m in range(packs)], [w.dy.at[m] for m in range(packs)])
            emit(s, number, lambda slot: put(slot, value))
            if number % 3 == 2:
                ticks(spread)
        settle_stores()
        ready[0] = (0 if s else count) + 2 * (inner // block)

    def lift_weights(s, spread):
        for m in range(packs):
            got(("mixed", m))
        number = inner // block
        for column in range(0, inner, width):
            for first in range(0, width, block):
                value = product(
                    [w.narrow.at[m, :, pl.ds(first, block)] for m in range(packs)],
                    [w.wide_b.at[m, :, pl.ds(column, width)] for m in range(packs)],
                )
                emit(s, number, lambda slot: put(slot, value))
                number += 1
                if number % 3 == 0:
                    ticks(spread)
        settle_stores()
        ready[0] = (0 if s else count) + 2 * number
        for m in range(packs):
            ask(("qkvc", m), kept[s].qkvc.at[m], w.wide_a.at[m])
            ask(("normed", m), kept[s].normed.at[m], w.narrow.at[m])
            if s:
                ask(("source", m), kept[s].source.at[m], w.source.at[m])
        ask_e(s, 0)

    def e_copy(s, number):
        m, pair = divmod(number, pairs)
        return pltpu.make_async_copy(
            kept[s].e.at[m, pl.ds(2 * pair, 2)], w.e.at[number % 2], w.e_load.at[number % 2]
        )

    def ask_e(s, number):
        if number < packs * pairs:
            e_copy(s, number).start()

    def attention(s, m, spread, between=None):
        if m == 0:
            got("out")
        got(("middle", m))
        if s:
            got(("ends", m))
            for r in range(0, rows, 32):
                at = pl.ds(r, 32)
                mine = w.middle[m, pl.ds(pl.multiple_of(own + r, 32), 32)]
                w.ends[m, at] = mine + wide(w.ends_mine[m, at]) + small[1, pl.ds(5, 1)]
        dm[s][m].wait()
        totals = [0.0, 0.0, 0.0]
        for at in row_blocks(every, 32):
            grad = wide(w.dm_mine[m, at]) + wide(w.dm_peer[m, at])
            pulled, along = norm_rows_back(w.middle[m, at], grad, small[s, pl.ds(1, 1)])
            through = wide(w.dy[m, at]) + pulled
            w.dmid[m, at] = through
            da = low(through)
            w.da[m, at] = da
            for i, piece in enumerate((along, grad, wide(da))):
                totals[i] = totals[i] + column_sum(piece)
        for i, row in enumerate((1, 3, 4)):
            add_sums(s, m, row, 0.5 * totals[i])
        ticks(1)
        got(("inv", m))
        w.dc[...] = dot(w.da[m], w.out[...], across) * w.inv[m]
        got(("qkvc", m))
        for pair in range(pairs):
            number = m * pairs + pair
            e_copy(s, number).wait()
            ask_e(s, number + 1)
            e_ref = w.e.at[number % 2]

            def lanes(i):
                return pl.ds(i * part + pair * 2 * HEAD_DIM, 2 * HEAD_DIM)

            queries, keys, values = (w.wide_a[m, :, lanes(i)] for i in range(3))
            grad = low(w.dc[:, lanes(0)])
            for side in range(2):
                here = early if side == 0 else jnp.logical_not(early)
                w.dprob[side] = dot(jnp.where(here, grad, 0), values, across)
            for side in range(2):
                here = early if side == 0 else jnp.logical_not(early)
                for at in row_blocks(every):
                    level = jnp.where(here, w.dc[at, lanes(0)] * wide(w.wide_a[m, at, lanes(3)]), 0.0)
                    level = jnp.sum(level, axis=-1, keepdims=True)
                    w.ds[side, at] = low(wide(e_ref[side, at]) * (w.dprob[side, at] - level))
            dv = [dot(e_ref[side], grad, down) for side in range(2)]
            w.wide_b[m, :, lanes(2)] = low(jnp.where(early, dv[0], dv[1]))
            dk = [dot(w.ds[side], queries, down) for side in range(2)]
            w.wide_b[m, :, lanes(1)] = low(jnp.where(early, dk[0], dk[1]))
            dq = [dot(w.ds[side], keys) for side in range(2)]
            w.wide_b[m, :, lanes(0)] = low(SCALE * jnp.where(early, dq[0], dq[1]))
            ticks(spread)
            if between is not None and pair == 0:
                between()
        if m == 0:
            got("joint")
        if s == 0:
            dn[1][m].wait_send()
        for r in (0, rows):
            at = pl.ds(r, rows)
            dq, dk, dv = (w.wide_b[m, at, pl.ds(i * part, part)] for i in range(3))
            far = dot(dk, w.joint[1], across) + dot(dv, w.joint[2], across)
            near = dot(dq, w.joint[0], across)
            if s:
                w.dm_mine[m, at] = low(far)
                w.middle[m, at] = near + jnp.where(core == 0, far, 0.0)
            else:
                w.dn_mine[m, at] = low(near + far)
        if s:
            pl.when(core == 1)(lambda: far_copy(m).start())
        else:
            dn[0][m].start()

    def join(m):
        pl.when(core == 0)(lambda: far_copy(m).wait_recv())
        for at in row_blocks(every, 32):
            there = jnp.where(core == 0, wide(w.crossed[m, at]), 0.0)
            w.dn_mine[m, at] = low(w.middle[m, at] + there)
        dn[1][m].start()

    def attention_weights(s, spread):
        for m in range(packs):
            got(("normed", m))
            if s:
                got(("source", m))
        normed = [w.narrow.at[m] for m in range(packs)]
        source = [w.source.at[m] for m in range(packs)] if s else normed
        dq, dk, dv = (
            [w.wide_b.at[m, :, pl.ds(i * part, part)] for m in range(packs)] for i in range(3)
        )
        context = [w.wide_a.at[m, :, pl.ds(3 * part, part)] for m in range(packs)]
        da = [w.da.at[m] for m in range(packs)]
        number = 2 * inner // block
        for first in range(0, width, block):
            at = pl.ds(first, block)
            query = product([n.at[:, at] for n in normed], dq)
            key = product([n.at[:, at] for n in source], dk)

            def both(slot):
                put(slot, query, 0, pl.ds(0, part))
                put(slot, key, 0, pl.ds(part, part))

            emit(s, number, both)
            number += 1
            ticks(spread)
        size = 128
        per = block // size
        strips = [("value", r) for r in range(0, part, size)] + [("out", r) for r in range(0, part, size)]
        for first in range(0, len(strips), per):
            group = strips[first : first + per]

            def fill(slot):
                for i, (kind, r) in enumerate(group):
                    if kind == "value":
                        for side in range(width // part):
                            at = pl.ds(side * part + r, size)
                            value = product([n.at[:, at] for n in source], dv)
                            put(slot, value, i * size, pl.ds(side * part, part))
                    else:
                        value = product([c.at[:, pl.ds(r, size)] for c in context], da)
                        put(slot, value, i * size)

            emit(s, number, fill)
            number += 1
            ticks(spread)
        settle_stores()
        ready[0] = (0 if s else count) + 2 * number

    def leave(s, m):
        dn[s][m].wait_recv()
        got(("base", m))
        totals = [0.0, 0.0]
        for r in range(0, every if s else rows, 32):
            peer, mine = pl.ds(r, 32), pl.ds(r if s else pl.multiple_of(own + r, 32), 32)
            grad = wide(w.dn_mine[m, mine]) + wide(w.dn_peer[m, peer])
            pulled, along = norm_rows_back(wide(w.base[m, peer]), grad, small[s, pl.ds(0, 1)])
            result = low(w.dmid[m, mine] + pulled)
            if s:
                w.dy[m, peer] = result
            else:
                w.dx[m, peer] = result
            for i, piece in enumerate((along, grad)):
                totals[i] = totals[i] + column_sum(piece)
        scale = 0.5 if s else 1.0
        add_sums(s, m, 0, scale * totals[0])
        add_sums(s, m, 2, scale * totals[1])

    def vectors(s):
        return remote(w.sums.at[s], w.sums_peer.at[s], w.v_send.at[s], w.v_recv.at[s], x_peer)

    def tail_store(s):
        return pltpu.make_async_copy(w.tail, g_refs[s].at[count - 1], w.t_store.at[s])

    def finish_vectors(s):
        vectors(s).wait()
        row = lax.broadcasted_iota(jnp.int32, (8, 1), 0)
        total = w.sums[s] + jnp.where(row < VECTORS, w.sums_peer[s], 0.0)
        if s:
            w.tail[...] = jnp.zeros(w.tail.shape, w.tail.dtype)
        pad = jnp.zeros((w.tail.shape[1] - 8, width), jnp.float32)
        w.tail[0] = low(jnp.concatenate([total, pad]))
        tail_store(s).start()
        tail_store(s).wait()
        ready[0] = count if s else 2 * count

    def ends_copy(m):
        return remote(
            y_in.at[m, pl.ds(theirs, rows)], w.ends_peer.at[m], w.y_send.at[m], w.y_recv.at[m], x_peer
        )

    def ends(m):
        ends_copy(m).wait()
        for at in row_blocks(rows, 32):
            w.ends_mine[m, at] = low(w.ends[m, at] + wide(w.ends_peer[m, at]))

    def edges_keep(src, b):
        return pltpu.make_async_copy(src, edges_ref.at[b], w.o_keep.at[0])

    def edges_hand(src, b):
        return remote(src, edges_ref.at[b], w.o_send.at[0], w.o_recv.at[0], sibling)

    def ask_base(s):
        for m in range(packs):
            if s:
                ask(("base", m), kept[s].base.at[m], w.base.at[m])
            else:
                ask(("base", m), kept[s].base.at[m, pl.ds(own, rows)], w.base.at[m, pl.ds(0, rows)])

    for s in (1, 0):
        if s:
            for m in range(packs):
                got(("dy", m))
            drop_weights(1, 0)
        got("drop")
        got("lift")
        for m in range(packs):
            feed_forward(s, m)
            ticks(1)
        if s == 0:
            finish_vectors(1)
            for m in range(packs):
                ends(m)
            pl.when(core == 0)(lambda: edges_hand(w.ends_mine, 0).start())
            pl.when(core == 1)(lambda: edges_keep(w.ends_mine, 1).start())
            drop_weights(0, 1)
        ask_base(s)
        if s:
            ask_layer(0)
            for m in range(packs):
                ends_copy(m).start()
        lift_weights(s, 1)
        for m in range(packs):
            attention(s, m, 2, partial(join, m - 1) if s and m else None)
        if s:
            join(packs - 1)
            ask_attention(0)
        attention_weights(s, 1)
        if s:
            ask_rows(0)
        for m in range(packs):
            leave(s, m)
            ticks(1)
        vectors(s).start()
    finish_vectors(0)
    pl.when(core == 0)(lambda: edges_keep(w.dx, 0).start())
    pl.when(core == 1)(lambda: edges_hand(w.dx, 1).start())
    if inside:
        run_ticks(clock[0], length)
        drain()
    for m in range(packs):
        dn[0][m].wait_send()
    edges_keep(w.dx, 0).wait()
    edges_hand(w.dx, 0).wait()


def backward(line, small, dy, ends, weights, kept, inside):
    packs, every, width = dy.shape
    rows = every // 2
    inner, part = weights[0][0].shape[0], weights[0][3].shape[0]
    block = 8 * CHUNK
    count = (2 * inner + 4 * part) // (4 * CHUNK) + 1
    chunks = shape((count, 4, CHUNK, width))
    args = [small, dy, ends] + [a for s in range(2) for a in weights[s]] + [a for s in range(2) for a in kept[s]]
    anywhere = pl.BlockSpec(memory_space=pl.ANY)
    outs = [shape((2, packs, rows, width)), chunks, chunks]
    if inside:
        outs.append(shape((2,) + chunks.shape))
    names, scratch = backward_scratch(packs, rows, width, part, inner, block)
    if inside:
        bufs, sems = reducer_scratch(line, CHUNK, width)
        scratch = scratch + bufs + sems
    return pl.pallas_call(
        partial(backward_kernel, line, count, packs, inside, names),
        out_shape=outs,
        in_specs=[pl.BlockSpec(memory_space=pltpu.VMEM)] + [anywhere] * (len(args) - 1),
        out_specs=[anywhere] * len(outs),
        scratch_shapes=scratch,
        compiler_params=pltpu.CompilerParams(
            collective_id=2, has_side_effects=True, vmem_limit_bytes=62 * 1024 * 1024
        ),
    )(*args)


def local(
    edges_in,
    joint_weight,
    output_weight,
    lift_weight,
    lift_bias,
    drop_weight,
    norm_gains,
    norm_shifts,
    branch_biases,
    item_lengths,
    key_keep,
):
    half = lax.axis_index("tensor")
    held = edges_in[0]
    packs, _, width = held.shape[1:]
    part = joint_weight.shape[-1]
    inner = lift_weight.shape[-1]
    heads = part // HEAD_DIM
    head_ids = wide(half * heads + jnp.arange(heads, dtype=jnp.int32))
    slopes = jnp.power(2.0, -8.0 * (head_ids + 1.0) / HEADS)

    small = jnp.concatenate(
        [norm_gains[0], norm_shifts[0], branch_biases[0], lift_bias[0].reshape(2, -1, width)], axis=1
    )
    small = jnp.concatenate([small, jnp.zeros((2, 16 - small.shape[1], width), small.dtype)], axis=1)
    distances = [masked_distance(item_lengths[0, m], key_keep[0, m]) for m in range(packs)]
    given = (joint_weight[0], output_weight[0], small, lift_weight[0], drop_weight[0])
    kept, weights, small, dy, ends = forward(slopes, held, distances, given)
    line = lax.axis_size("dp") // 2
    inside = line == 4
    edges_out, *grads = backward(line, small, dy, ends, weights, kept, inside)
    grads = grads[2] if inside else reduce_over_dp(grads, line)
    grads = grads.reshape(2, -1, width)
    weight_rows = 2 * inner + 4 * part
    drop_grad, lift_grad, joint_grad, output_grad = widened(grads, inner, part)
    vectors = wide(grads[:, weight_rows : weight_rows + 6])
    lift_total = wide(grads[:, weight_rows + 6 : weight_rows + 6 + inner // width]).reshape(2, inner)
    return (
        edges_out[None],
        joint_grad[None],
        output_grad[None],
        lift_grad[None],
        lift_total[None],
        drop_grad[None],
        vectors[None, :, 0:2],
        vectors[None, :, 2:4],
        vectors[None, :, 4:6],
    )


def solution(mesh):
    in_specs = (
        P("section", None, None, ("dp", "tensor"), None),
        P("section", None, None, None, "tensor"),
        P("section", None, "tensor", None),
        P("section", None, None, "tensor"),
        P("section", None, "tensor"),
        P("section", None, "tensor", None),
        P("section", None, None, None),
        P("section", None, None, None),
        P("section", None, None, None),
        P("dp", None, None),
        P("dp", None, None),
    )
    out_specs = (
        P("section", None, None, ("dp", "tensor"), None),
        P("section", None, None, None, "tensor"),
        P("section", None, "tensor", None),
        P("section", None, None, "tensor"),
        P("section", None, "tensor"),
        P("section", None, "tensor", None),
        P("section", None, None, None),
        P("section", None, None, None),
        P("section", None, None, None),
    )
    return jax.shard_map(local, mesh=mesh, in_specs=in_specs, out_specs=out_specs, check_vma=False)
```

```python
from functools import partial

import jax
import jax.numpy as jnp
from jax import lax
from jax.experimental import pallas as pl
from jax.experimental.pallas import tpu as pltpu
from jax.sharding import PartitionSpec as P

HEADS = 12
HEAD_DIM = 64
EPSILON = 1e-06
SCALE = HEAD_DIM ** (-0.5)
FAR = 1e30
CHUNK = 48
AHEAD = 2
HOP = 2
VMEM_LIMIT = 44 * 1024 * 1024
MESH = pl.DeviceIdType.MESH


def swap(value, axis):
    return lax.ppermute(value, axis, [(0, 1), (1, 0)])


def pick(stacked, index, axis=0):
    return lax.dynamic_index_in_dim(stacked, index, axis, keepdims=False)


def masked_distance(lengths, keep_row):
    rows_all = keep_row.shape[0]
    slots = lengths.shape[0]
    positions = jnp.arange(rows_all, dtype=jnp.int32)
    ends = jnp.cumsum(lengths)
    segment = jnp.sum((positions[:, None] >= ends[None, :]).astype(jnp.int32), axis=1)
    following = jnp.arange(1, slots + 1, dtype=jnp.int32)
    item_ids = jnp.arange(slots, dtype=jnp.int32)
    begin = jnp.sum(jnp.where(segment[:, None] == following[None, :], ends[None, :], 0), axis=1)
    length = jnp.sum(jnp.where(segment[:, None] == item_ids[None, :], lengths[None, :], 0), axis=1)
    side = jnp.where(length == 144, 12, jnp.where(length == 225, 15, 20)).astype(jnp.int32)
    offset = positions - begin
    grid_row = (offset // side).astype(jnp.float32)
    column = (offset % side).astype(jnp.float32)
    row_gap = grid_row[:, None] - grid_row[None, :]
    col_gap = column[:, None] - column[None, :]
    distance = jnp.sqrt(row_gap * row_gap + col_gap * col_gap)
    allowed = (segment[:, None] == segment[None, :]) & (
        (keep_row[None, :] == 1) | (positions[:, None] == positions[None, :])
    )
    return jnp.where(allowed, distance, FAR)


def dot(a, b, dims=((1,), (0,))):
    return lax.dot_general(a, b, (dims, ((), ())), preferred_element_type=jnp.float32)


def low(value):
    return value.astype(jnp.bfloat16)


def wide(value):
    return value.astype(jnp.float32)


def shape(dims, dtype=jnp.bfloat16):
    return jax.ShapeDtypeStruct(tuple(dims), dtype)


def row_blocks(count, size=64):
    return [pl.ds(r, size) for r in range(0, count, size)]


def norm_rows(values, gain, shift):
    mean = jnp.mean(values, axis=-1, keepdims=True)
    centred = values - mean
    variance = jnp.mean(centred * centred, axis=-1, keepdims=True)
    return centred * lax.rsqrt(variance + EPSILON) * gain + shift


def norm_rows_back(values, grad, gain):
    mean = jnp.mean(values, axis=-1, keepdims=True)
    centred = values - mean
    variance = jnp.mean(centred * centred, axis=-1, keepdims=True)
    spread = lax.rsqrt(variance + EPSILON)
    unit = centred * spread
    scaled = grad * gain
    along = jnp.mean(scaled * unit, axis=-1, keepdims=True)
    level = jnp.mean(scaled, axis=-1, keepdims=True)
    return spread * (scaled - level - unit * along), grad * unit


def column_sum(value):
    return jnp.sum(value, axis=0, keepdims=True)


def widen_kernel(
    each, g_ref, drop, lift, joint, out, gains, shifts, biases, lift_bias,
    held, square, triple, last, thin, load_sem, thin_sem, store_sem,
):
    streams, _, width = g_ref.shape
    part = out.shape[1]
    blocks = 2 * each + 2

    def load(b, i):
        return pltpu.make_async_copy(
            g_ref.at[b, pl.ds(i * width, width)], held.at[b, i], load_sem.at[b, i]
        )

    def store(b, i):
        if i < each:
            src, dst = square.at[b, i], drop.at[b, pl.ds(i * width, width)]
        elif i < 2 * each:
            src, dst = square.at[b, i], lift.at[b, :, pl.ds((i - each) * width, width)]
        elif i == 2 * each:
            src, dst = triple.at[b, pl.ds(0, 2)], joint.at[b, pl.ds(0, 2)]
        else:
            src, dst = triple.at[b, 2], joint.at[b, 2]
        return pltpu.make_async_copy(src, dst, store_sem.at[b, i])

    def store_out(b):
        return pltpu.make_async_copy(last.at[b], out.at[b], store_sem.at[b, blocks])

    def load_thin(b):
        return pltpu.make_async_copy(
            g_ref.at[b, pl.ds(blocks * width, thin.shape[1])], thin.at[b], thin_sem.at[b]
        )

    every = [(b, i) for i in range(blocks) for b in range(streams)]
    for b, i in every:
        load(b, i).start()
    for b in range(streams):
        load_thin(b).start()
    size = 64
    for b, i in every:
        load(b, i).wait()
        if i < 2 * each:

            @pl.loop(0, width // size)
            def _(r):
                at = pl.ds(pl.multiple_of(r * size, size), size)
                square[b, i, at] = wide(held[b, i, at])

        elif i == 2 * each:

            @pl.loop(0, width // size)
            def _(r):
                at = pl.ds(pl.multiple_of(r * size, size), size)
                for n in range(2):
                    triple[b, n, at] = wide(held[b, i, at, pl.ds(n * part, part)])

        else:

            @pl.loop(0, part // size)
            def _(r):
                at = pl.ds(pl.multiple_of(r * size, size), size)
                low_at = pl.ds(pl.multiple_of(part + r * size, size), size)
                triple[b, 2, at] = wide(held[b, i, at, pl.ds(0, part)])
                triple[b, 2, low_at] = wide(held[b, i, at, pl.ds(part, part)])
                last[b, at] = wide(held[b, i, low_at])

            store_out(b).start()
        store(b, i).start()
    for b in range(streams):
        load_thin(b).wait()
        rows = wide(thin[b])
        for i, ref in enumerate((gains, shifts, biases)):
            ref[b] = rows[2 * i : 2 * i + 2]
        for i in range(each):
            lift_bias[b : b + 1, pl.ds(i * width, width)] = rows[VECTORS + i : VECTORS + i + 1]
    for b, i in every:
        store(b, i).wait()
    for b in range(streams):
        store_out(b).wait()


def widened(grads, inner, part):
    streams, _, width = grads.shape
    each = inner // width
    f32 = jnp.float32
    outs = [(streams, inner, width), (streams, width, inner), (streams, 3, width, part), (streams, part, width)]
    outs += [(streams, 2, width)] * 3 + [(streams, inner)]
    anywhere = pl.BlockSpec(memory_space=pl.ANY)
    return pl.pallas_call(
        partial(widen_kernel, each),
        in_specs=[anywhere],
        out_specs=[anywhere] * 4 + [pl.BlockSpec(memory_space=pltpu.VMEM)] * 4,
        out_shape=[shape(dims, f32) for dims in outs],
        scratch_shapes=[
            pltpu.VMEM((streams, 2 * each + 2, width, width), jnp.bfloat16),
            pltpu.VMEM((streams, 2 * each, width, width), f32),
            pltpu.VMEM(outs[2], f32),
            pltpu.VMEM(outs[3], f32),
            pltpu.VMEM((streams, 16, width), jnp.bfloat16),
            pltpu.SemaphoreType.DMA((streams, 2 * each + 2)),
            pltpu.SemaphoreType.DMA((streams,)),
            pltpu.SemaphoreType.DMA((streams, 2 * each + 3)),
        ],
        compiler_params=pltpu.CompilerParams(vmem_limit_bytes=52 * 1024 * 1024),
    )(grads)


class Names:
    def __init__(self, pairs):
        for name, ref in pairs:
            setattr(self, name, ref)


KEPT = tuple(dict(qkvc=0, e=0, inv=0, normed=0, source=0, middle=0, mixed=0, act=0, steep=0, base=0))
WEIGHTS = tuple(dict(drop=0, lift=0, joint=0, out=0))
GIVEN = tuple(dict(joint=0, out=0, small=0, lift=0, drop=0))
VECTORS = 6
LOADS = 64


def kept_shapes(s, packs, every, width, part, inner):
    heads = part // HEAD_DIM
    f32 = jnp.float32
    dims = dict(
        qkvc=shape((packs, every, 4 * part)),
        e=shape((packs, heads, every, every)),
        inv=shape((packs, every, part), f32),
        normed=shape((packs, every, width)),
        source=shape((packs, every, width)),
        middle=shape((packs, every, width), f32),
        mixed=shape((packs, every, width)),
        act=shape((packs, every, inner)),
        steep=shape((packs, every, inner)),
        base=shape((packs, every, width)),
    )
    if s == 0:
        dims.pop("source")
    return dims


def forward_plan(packs, every, width, part, inner):
    full, f32, bf16 = (packs, every, width), jnp.float32, jnp.bfloat16
    rooms = dict(
        joint=((2, 3, width, part), bf16),
        out=((2, part, width), bf16),
        small_in=((2, 16, width), bf16),
        lift=((2, width, inner), bf16),
        drop=((2, inner, width), bf16),
        dist=((packs, every, every), f32),
        rows_in=(full, bf16),
        base=(full, bf16),
        dy=(full, bf16),
        normed=(full, bf16),
        crossed=(full, bf16),
        source=(full, bf16),
        qkvc=((packs, every, 4 * part), bf16),
        e=((part // HEAD_DIM, every, every), bf16),
        inv=((packs, every, part), f32),
        a_mine=(full, bf16),
        a_peer=(full, bf16),
        y_mine=(full, bf16),
        y_peer=(full, bf16),
        middle=(full, f32),
        mixed=(full, bf16),
        act=((packs, every, inner), bf16),
        steep=((packs, every, inner), bf16),
        scores=((2, every, every), f32),
        hidden=((2, every, 256), f32),
    )
    sem = pltpu.SemaphoreType.DMA
    flags = dict(
        w_load=sem((5,)),
        w_send=sem((5,)),
        w_recv=sem((5,)),
        d_load=sem((packs,)),
        r_load=sem((2, packs)),
        r_send=sem((2, 2, 2, packs)),
        r_recv=sem((2, 2, packs)),
        x_send=sem((2, 2, packs)),
        x_recv=sem((2, 2, packs)),
        c_send=sem((packs,)),
        c_recv=sem((packs,)),
        store=sem((LOADS,)),
    )
    scratch = [pltpu.VMEM(*spec) for spec in rooms.values()] + list(flags.values())
    return list(rooms) + list(flags), scratch


def forward_kernel(packs, names, *refs):
    refs = list(refs)

    def take(n):
        taken = refs[:n]
        del refs[:n]
        return taken

    slopes, rows_ref = take(2)
    dist_refs = take(packs)
    given = dict(zip(GIVEN, take(5)))
    kept = [
        Names(zip([k for k in KEPT if s or k != "source"], take(len(KEPT) - (s == 0)))) for s in range(2)
    ]
    placed = [Names(zip(WEIGHTS, take(4))) for _ in range(2)]
    small_ref, dy_ref, y_ref = take(3)
    w = Names(zip(names, refs))
    core, half = lax.axis_index("section"), lax.axis_index("tensor")
    away = 1 - half
    every, width = w.base.shape[1:]
    rows = every // 2
    part, inner = w.out.shape[1], w.drop.shape[1]
    own = pl.ds(pl.multiple_of(half * rows, rows), rows)
    x_peer = {"tensor": away}
    sibling = {"section": 1 - core}
    early = lax.broadcasted_iota(jnp.int32, (1, 2 * HEAD_DIM), 1) < HEAD_DIM
    across = ((1,), (1,))

    def remote(src, dst, sent, got, target):
        return pltpu.make_async_remote_copy(
            src_ref=src, dst_ref=dst, send_sem=sent, recv_sem=got,
            device_id=target, device_id_type=MESH,
        )

    def weight_load(i):
        return pltpu.make_async_copy(
            given[GIVEN[i]].at[core], getattr(w, room[i]).at[core], w.w_load.at[i]
        )

    def weight_out(i):
        return remote(
            given[GIVEN[i]].at[1 - core], getattr(w, room[i]).at[core], w.w_send.at[i], w.w_recv.at[i], sibling
        )

    def dist_load(m):
        return pltpu.make_async_copy(dist_refs[m], w.dist.at[m], w.d_load.at[m])

    room = tuple("small_in" if name == "small" else name for name in GIVEN)
    lands = (w.rows_in, w.dy)

    def rows_load(kind, m):
        return pltpu.make_async_copy(rows_ref.at[kind, m], lands[kind].at[m, own], w.r_load.at[kind, m])

    def rows_out(kind, b, t, m):
        side = jnp.where(t == half, 0, 1)
        return remote(
            rows_ref.at[b, m], lands[kind].at[m, own], w.r_send.at[kind, b, side, m], w.r_recv.at[kind, side, m],
            {"section": b, "tensor": t},
        )

    def rows_start(kind, m):
        @pl.when(core == kind)
        def _():
            rows_out(kind, 1 - kind, away, m).start()
            rows_out(kind, kind, away, m).start()
            rows_out(kind, 1 - kind, half, m).start()

    def rows_got(kind, m):
        rows_out(kind, 0, away, m).wait_recv()

        @pl.when(core == kind)
        def _():
            rows_load(kind, m).wait()

        @pl.when(core != kind)
        def _():
            rows_out(kind, 0, half, m).wait_recv()

    def rows_sent(kind, m):
        @pl.when(core == kind)
        def _():
            rows_out(kind, 1 - kind, away, m).wait_send()
            rows_out(kind, kind, away, m).wait_send()
            rows_out(kind, 1 - kind, half, m).wait_send()

    for i in range(len(room)):
        weight_load(i).start()
    for m in range(packs):
        dist_load(m).start()
        for kind in range(2):
            pl.when(core == kind)(lambda: rows_load(kind, m).start())
    barrier = pltpu.get_barrier_semaphore()
    for c, t in [(1 - core, half), (core, away), (1 - core, away)]:
        pl.semaphore_signal(
            barrier, inc=1, device_id={"section": c, "tensor": t}, device_id_type=MESH
        )
    pl.semaphore_wait(barrier, 3)
    rows_start(0, 0)
    for i in range(3):
        weight_out(i).start()
    for m in range(1, packs):
        rows_start(0, m)
    for i in range(3, len(room)):
        weight_out(i).start()

    numbers = iter(range(LOADS))
    pending = {}

    def store(key, src, dst):
        copy = pltpu.make_async_copy(src, dst, w.store.at[next(numbers)])
        copy.start()
        pending[key] = copy

    def free(*key):
        if key in pending:
            pending.pop(key).wait()

    def keep(name, s, m):
        store((name, m), getattr(w, name).at[m], getattr(kept[s], name).at[m])

    def weight_got(name, s):
        i = room.index(name)
        pl.when(core == s)(lambda: weight_load(i).wait())
        pl.when(core != s)(lambda: weight_out(i).wait_recv())
        if name in WEIGHTS:
            store((name, "placed", s), getattr(w, name).at[s], getattr(placed[s], name))

    vectors = [None, None]

    def small_got(s):
        weight_got("small_in", s)
        vectors[s] = wide(w.small_in[s])
        small_ref[s] = vectors[s]

    def row(s, i):
        return vectors[s][i : i + 1]

    def over_x(src, dst, kind, s, m):
        return remote(src, dst, w.x_send.at[kind, s, m], w.x_recv.at[kind, s, m], x_peer)

    def a_copy(s, m):
        return over_x(w.a_mine.at[m], w.a_peer.at[m], 0, s, m)

    def y_copy(m):
        return over_x(w.y_mine.at[m], w.y_peer.at[m], 1, 0, m)

    def crossing(m):
        return remote(w.normed.at[m], w.crossed.at[m], w.c_send.at[m], w.c_recv.at[m], sibling)

    def attention(s, m):
        source = w.source if s else w.normed
        free("qkvc", m)
        w.qkvc[m, :, pl.ds(0, part)] = low(SCALE * dot(w.normed[m], w.joint[s, 0]))
        if s:

            @pl.when(core == 0)
            def _():
                w.source[m] = w.normed[m]

            @pl.when(core == 1)
            def _():
                crossing(m).wait_recv()
                w.source[m] = w.crossed[m]

            keep("source", s, m)
        for i in (1, 2):
            w.qkvc[m, :, pl.ds(i * part, part)] = low(dot(source[m], w.joint[s, i]))
        if s == 0:
            dist_load(m).wait()
        free("inv", m)
        free("e")

        @pl.loop(0, part // (2 * HEAD_DIM))
        def _(pair):
            def lanes(i):
                start = i * part + pair * 2 * HEAD_DIM
                return pl.ds(pl.multiple_of(start, 2 * HEAD_DIM), 2 * HEAD_DIM)

            queries, keys, values = (w.qkvc[m, :, lanes(i)] for i in range(3))
            for side in range(2):
                here = early if side == 0 else jnp.logical_not(early)
                w.scores[side] = dot(jnp.where(here, queries, 0), keys, across)
            for side in range(2):
                head = 2 * pair + side
                here = early if side == 0 else jnp.logical_not(early)
                slope = slopes[head]
                for at in row_blocks(every):
                    value = w.scores[side, at] - slope * w.dist[m, at]
                    expo = jnp.exp(value - jnp.max(value, axis=-1, keepdims=True))
                    w.e[head, at] = low(expo)
                    inverse = 1.0 / jnp.sum(expo, axis=-1, keepdims=True)
                    if side == 0:
                        w.inv[m, at, lanes(0)] = jnp.broadcast_to(inverse, (64, 2 * HEAD_DIM))
                    else:
                        w.inv[m, at, lanes(0)] = jnp.where(here, inverse, w.inv[m, at, lanes(0)])
            sums = [dot(w.e[2 * pair + side], values) for side in range(2)]
            context = jnp.where(early, sums[0], sums[1]) * w.inv[m, :, lanes(0)]
            w.qkvc[m, :, lanes(3)] = low(context)

        if m == 0:
            weight_got("out", s)
        if s:
            a_copy(0, m).wait_send()
        for r in (0, rows):
            at = pl.ds(r, rows)
            w.a_mine[m, at] = low(dot(w.qkvc[m, at, pl.ds(3 * part, part)], w.out[s]))
        a_copy(s, m).start()
        store(("e",), w.e, kept[s].e.at[m])
        keep("qkvc", s, m)
        keep("inv", s, m)

    def feed_forward(s, m):
        base = w.base if s else w.rows_in
        a_copy(s, m).wait_recv()
        for name in ("middle", "mixed", "act", "steep"):
            free(name, m)
        for at in row_blocks(every):
            total = wide(w.a_mine[m, at]) + wide(w.a_peer[m, at])
            value = wide(base[m, at]) + total + row(s, 4)
            w.middle[m, at] = value
            w.mixed[m, at] = low(norm_rows(value, row(s, 1), row(s, 3)))
        if m == 0:
            weight_got("lift", s)
            weight_got("drop", s)
        size = w.hidden.shape[-1]
        for number in range(inner // size):
            lanes = pl.ds(number * size, size)
            at, off = divmod(number * size, width)
            bias = vectors[s][VECTORS + at : VECTORS + at + 1, off : off + size]
            w.hidden[number % 2] = dot(w.mixed[m], w.lift[s, :, lanes])
            for at in row_blocks(every):
                value = w.hidden[number % 2, at] + bias
                below = 0.5 + 0.5 * lax.erf(value * (0.5**0.5))
                density = 0.3989422804014327 * jnp.exp(-0.5 * value * value)
                w.act[m, at, lanes] = low(value * below)
                w.steep[m, at, lanes] = low(below + value * density)
        if s:
            y_copy(m).wait_send()
        for r in (0, rows):
            at = pl.ds(r, rows)
            w.y_mine[m, at] = low(dot(w.act[m, at], w.drop[s]))
        if s == 0:
            y_copy(m).start()
        else:
            store(("y", m), w.y_mine.at[m], y_ref.at[m])
        for name in ("middle", "mixed", "act", "steep"):
            keep(name, s, m)

    def enter(m):
        y_copy(m).wait_recv()
        free("normed", m)
        for at in row_blocks(every):
            total = wide(w.y_mine[m, at]) + wide(w.y_peer[m, at])
            value = low(w.middle[m, at] + total + row(0, 5))
            w.base[m, at] = value
            w.normed[m, at] = low(norm_rows(wide(value), row(1, 0), row(1, 2)))
        pl.when(core == 0)(lambda: crossing(m).start())
        keep("base", 1, m)
        keep("normed", 1, m)

    small_got(0)
    weight_got("joint", 0)
    for m in range(packs):
        rows_got(0, m)
        for at in row_blocks(every):
            w.normed[m, at] = low(norm_rows(wide(w.rows_in[m, at]), row(0, 0), row(0, 2)))
        store(("rows", m), w.rows_in.at[m], kept[0].base.at[m])
        keep("normed", 0, m)
        attention(0, m)
    for m in range(packs):
        feed_forward(0, m)
    small_got(1)
    weight_got("joint", 1)
    for m in range(packs):
        enter(m)
        attention(1, m)
    for m in range(packs):
        rows_start(1, m)
    for m in range(packs):
        feed_forward(1, m)
    for m in range(packs):
        rows_got(1, m)
        store(("dy", m), w.dy.at[m], dy_ref.at[m])
    for i in range(len(room)):
        weight_out(i).wait_send()
    for m in range(packs):
        for kind in range(2):
            rows_sent(kind, m)
        a_copy(1, m).wait_send()
        pl.when(core == 0)(lambda: crossing(m).wait_send())
    for key in list(pending):
        free(*key)


def forward(slopes, held, distances, weights):
    packs, rows, width = held.shape[1:]
    every = 2 * rows
    part, inner = weights[1].shape[1], weights[4].shape[1]
    order = dict(zip(GIVEN, weights))
    kept = [kept_shapes(s, packs, every, width, part, inner) for s in range(2)]
    outs = list(kept[0].values()) + list(kept[1].values())
    outs += [shape(order[name].shape[1:]) for name in WEIGHTS] * 2
    outs += [shape((2, 16, width), jnp.float32), shape((packs, every, width)), shape((packs, every, width))]
    names, scratch = forward_plan(packs, every, width, part, inner)
    anywhere = pl.BlockSpec(memory_space=pl.ANY)
    out_specs = [anywhere] * len(outs)
    out_specs[-3] = pl.BlockSpec(memory_space=pltpu.VMEM)
    found = list(
        pl.pallas_call(
            partial(forward_kernel, packs, names),
            out_shape=outs,
            in_specs=[pl.BlockSpec(memory_space=pltpu.SMEM)] + [anywhere] * (6 + packs),
            out_specs=out_specs,
            scratch_shapes=scratch,
            compiler_params=pltpu.CompilerParams(
                collective_id=1, has_side_effects=True, vmem_limit_bytes=60 * 1024 * 1024
            ),
        )(slopes, held, *distances, *weights)
    )
    results = []
    for s in range(2):
        layer = {name: found.pop(0) for name in kept[s]}
        layer.setdefault("source", layer["normed"])
        results.append([layer[name] for name in KEPT])
    placed = [[found.pop(0) for _ in WEIGHTS] for _ in range(2)]
    return results, placed, *found


def reducer(line, count, g_refs, o_ref, bufs, sems):
    load_ring, loads_ring, from_y, from_prv, from_nxt, both, mid2, from_y2, res2 = bufs
    load_sem, y_send, y_recv, n_send, n_recv, p_send, p_recv, f_send = sems[:8]
    load2, n2_send, p2_recv, m2_recv, u2_send, u2_recv, a2_send, r2_recv, o2_send = sems[8:17]
    s_send, l_sem, s2_send, l2_sem, f_recv, d_recv, s_recv = sems[17:]
    dp = lax.axis_index("dp")
    core = lax.axis_index("section")
    y, z = dp % 2, dp // 2
    depth = line // 2 - 1
    left = z < line // 2
    step = jnp.where(left, 1, -1)
    edge = jnp.where(left, z, line - 1 - z)
    mine = jnp.where(left, 0, 1)
    total = 2 * count
    slots = from_y.shape[0]
    ring = load_ring.shape[0]
    inner = edge == depth
    outer = jnp.logical_not(inner)

    def device(z_at, y_at, core_at):
        return {"dp": z_at * 2 + y_at, "section": core_at}

    across = device(z, 1 - y, core)
    across_other = device(z, 1 - y, 1 - core)
    sibling = device(z, y, 1 - core)
    nxt = device(z + step, y, core)
    prv = device(z - step, y, core)

    def greet(extra):
        barrier = pltpu.get_barrier_semaphore()
        targets = [across, across_other, sibling, nxt] + extra
        for target in targets:
            pl.semaphore_signal(barrier, inc=1, device_id=target, device_id_type=MESH)

        @pl.when(edge > 0)
        def _():
            pl.semaphore_signal(barrier, inc=1, device_id=prv, device_id_type=MESH)

        pl.semaphore_wait(barrier, len(targets) + jnp.where(edge > 0, 1, 0))

    def send(src, dst, sent, got, target):
        return pltpu.make_async_remote_copy(
            src_ref=src,
            dst_ref=dst,
            send_sem=sent,
            recv_sem=got,
            device_id=target,
            device_id_type=MESH,
        )

    def plus(into, other):
        return (into.astype(jnp.float32) + other.astype(jnp.float32)).astype(into.dtype)

    def guarded(k, body):
        pl.when((k >= 0) & (k < total))(lambda: body(k))

    def by_layer(k, body):
        pl.when(k < count)(lambda: body(g_refs[1], k))
        pl.when(k >= count)(lambda: body(g_refs[0], k - count))

    def stays(k):
        return jnp.where(k < count, 1, 0) == core

    def place(k):
        return jnp.where(k < count, k, k - count)

    def load(k, g_ref=g_refs[0], j=0):
        return pltpu.make_async_copy(g_ref.at[j, y], load_ring.at[k % ring], load_sem.at[k % ring])

    def over_y(k, g_ref=g_refs[0], j=0):
        i = k % slots
        return send(g_ref.at[j, 1 - y], from_y.at[i], y_send.at[i], y_recv.at[i], across)

    def inward(k):
        i = k % slots
        return send(from_y.at[i], from_prv.at[i], n_send.at[i], p_recv.at[i], nxt)

    def middle(k):
        i = k % slots
        return send(from_y.at[i], from_nxt.at[i], n_send.at[i], n_recv.at[i], nxt)

    def outward(k):
        i = k % slots
        return send(from_nxt.at[i], from_nxt.at[i], p_send.at[i], n_recv.at[i], prv)

    def keep(k):
        i = k % slots
        return pltpu.make_async_copy(from_nxt.at[i], o_ref.at[core, place(k), y], l_sem.at[i])

    def hand(k):
        i = k % slots
        return send(from_nxt.at[i], o_ref.at[core, place(k), y], s_send.at[i], s_recv, sibling)

    def back_same(k):
        i = k % slots
        return send(from_nxt.at[i], o_ref.at[core, place(k), y], f_send.at[i], f_recv, across)

    def back_other(k):
        i = k % slots
        return send(from_nxt.at[i], o_ref.at[core, place(k), y], f_send.at[i], d_recv, across_other)

    def begin(k):
        def one(g_ref, j):
            over_y(k, g_ref, j).start()
            load(k, g_ref, j).start()

        by_layer(k, one)

    def pair(k):
        load(k).wait()
        over_y(k).wait()
        i = k % slots
        from_y[i] = plus(from_y[i], load_ring[k % ring])

    def pass_on(k):
        i = k % slots

        @pl.when(edge > 0)
        def _():
            inward(k).wait_recv()
            from_y[i] = plus(from_y[i], from_prv[i])

        pl.when(inner)(lambda: middle(k).start())
        pl.when(outer)(lambda: inward(k).start())

    def finish(k):
        i = k % slots
        middle(k).wait()

        @pl.when(inner)
        def _():
            from_nxt[i] = plus(from_nxt[i], from_y[i])

        pl.when(edge > 0)(lambda: outward(k).start())

        @pl.when(stays(k))
        def _():
            back_same(k).start()
            keep(k).start()

        @pl.when(jnp.logical_not(stays(k)))
        def _():
            back_other(k).start()
            hand(k).start()

    def loads(k, g_ref=g_refs[0], j=0, into=None):
        into = loads_ring.at[k % ring] if into is None else into
        return pltpu.make_async_copy(g_ref.at[j, pl.ds(2, 2)], into, load2.at[k % ring])

    def inwards(k):
        i = k % slots
        return send(both.at[i], both.at[i], n2_send.at[i], p2_recv.at[i], nxt)

    def halve(k):
        i = k % slots
        return send(both.at[i, 1 - mine], mid2.at[i], n2_send.at[i], m2_recv.at[i], nxt)

    def trade(k):
        i = k % slots
        return send(both.at[i, mine], from_y2.at[i], u2_send.at[i], u2_recv.at[i], across)

    def rejoin(k, q):
        i = k % slots
        return send(res2.at[i, q], res2.at[i, q], a2_send.at[i], r2_recv.at[i, q], nxt)

    def outwards(k, q):
        i = k % slots
        return send(res2.at[i, q], res2.at[i, q], o2_send.at[i, q], r2_recv.at[i, q], prv)

    def keep2(k, q):
        i = k % slots
        return pltpu.make_async_copy(
            res2.at[i, q], o_ref.at[core, place(k), 2 + q], l2_sem.at[i, q]
        )

    def hand2(k, q):
        i = k % slots
        return send(res2.at[i, q], o_ref.at[core, place(k), 2 + q], s2_send.at[i, q], s_recv, sibling)

    def spread(k, q):
        pl.when(edge > 0)(lambda: outwards(k, q).start())
        pl.when(stays(k))(lambda: keep2(k, q).start())
        pl.when(jnp.logical_not(stays(k)))(lambda: hand2(k, q).start())

    def begin2(k):
        def one(g_ref, j):
            pl.when(edge == 0)(lambda: loads(k, g_ref, j, both.at[k % slots]).start())
            pl.when(edge > 0)(lambda: loads(k, g_ref, j).start())

        by_layer(k, one)

    def pass_on2(k):
        i = k % slots
        loads(k).wait()

        @pl.when(edge > 0)
        def _():
            inwards(k).wait_recv()
            both[i] = plus(both[i], loads_ring[k % ring])

        pl.when(inner)(lambda: halve(k).start())
        pl.when(outer)(lambda: inwards(k).start())

    def trade2(k):
        i = k % slots
        halve(k).wait()
        both[i, mine] = plus(both[i, mine], mid2[i])
        trade(k).start()

    def settle2(k):
        i = k % slots
        trade(k).wait()
        res2[i, mine] = plus(both[i, mine], from_y2[i])
        rejoin(k, mine).start()
        spread(k, mine)

    def finish2(k):
        @pl.when(inner)
        def _():
            rejoin(k, 1 - mine).wait_recv()
            spread(k, 1 - mine)

        @pl.when(outer)
        def _():
            inwards(k).wait_send()
            for q in range(2):
                rejoin(k, q).wait_recv()
                spread(k, q)

    def retire(k):
        @pl.when(inner)
        def _():
            rejoin(k, mine).wait_send()

        @pl.when(edge > 0)
        def _():
            outward(k).wait_send()
            for q in range(2):
                outwards(k, q).wait_send()

        back_same(k).wait_send()

        @pl.when(stays(k))
        def _():
            keep(k).wait()
            for q in range(2):
                keep2(k, q).wait()

        @pl.when(jnp.logical_not(stays(k)))
        def _():
            hand(k).wait_send()
            for q in range(2):
                hand2(k, q).wait_send()

    span = AHEAD + HOP * (2 * depth + 3) + 1

    def ticks(first, last):
        @pl.loop(first, last)
        def _(tick):
            now = tick - AHEAD
            guarded(tick - span, retire)
            guarded(tick, begin)
            guarded(now, pair)
            guarded(tick - HOP * edge, begin2)
            guarded(now - HOP * edge, pass_on)
            guarded(now - HOP * edge, pass_on2)

            @pl.when(inner)
            def _():
                guarded(now - HOP * (depth + 1), trade2)
                guarded(now - HOP * (depth + 2), settle2)

            guarded(now - HOP * (2 * depth + 1 - edge), finish)
            guarded(now - HOP * (2 * depth + 3 - edge), finish2)

    def drain():
        group = o_ref.at[0, :, 0]
        groups = o_ref.at[0, :, pl.ds(0, 3)]
        pltpu.make_async_copy(group, group, f_recv).wait()
        pltpu.make_async_copy(group, group, d_recv).wait()
        pltpu.make_async_copy(groups, groups, s_recv).wait()

    return greet, ticks, drain, total + span


def reducer_scratch(line, rows, width):
    slots = AHEAD + HOP * (line + 1) + 3
    ring = AHEAD + 1

    def room(*lead):
        return pltpu.VMEM(lead + (rows, width), jnp.bfloat16)

    def sems(*dims):
        return pltpu.SemaphoreType.DMA(dims)

    bufs = [room(ring), room(ring, 2)] + [room(slots)] * 3 + [room(slots, 2)]
    bufs += [room(slots)] * 2 + [room(slots, 2)]
    many, twice = sems(slots), sems(slots, 2)
    flags = [sems(ring)] + [many] * 7 + [sems(ring)] + [many] * 6 + [twice] * 2
    return bufs, flags + [many] * 2 + [twice] * 2 + [pltpu.SemaphoreType.DMA] * 3


BUFS, SEMS = 9, 24


def reduce_kernel(line, count, g_zero, g_one, o_ref, *refs):
    greet, ticks, drain, length = reducer(
        line, count, (g_zero, g_one), o_ref, refs[:BUFS], refs[BUFS:]
    )
    greet([])
    ticks(0, length)
    drain()


def reduce_over_dp(grads, line):
    count, _, rows, width = grads[0].shape
    bufs, sems = reducer_scratch(line, rows, width)
    return pl.pallas_call(
        partial(reduce_kernel, line, count),
        out_shape=shape((2,) + grads[0].shape),
        in_specs=[pl.BlockSpec(memory_space=pl.ANY)] * 2,
        out_specs=pl.BlockSpec(memory_space=pl.ANY),
        scratch_shapes=bufs + sems,
        compiler_params=pltpu.CompilerParams(
            collective_id=0, has_side_effects=True, vmem_limit_bytes=56 * 1024 * 1024
        ),
    )(*grads)


def backward_scratch(packs, rows, width, part, inner, block):
    full, f32 = (packs, 2 * rows, width), jnp.float32
    bf16 = jnp.bfloat16
    plan = dict(
        drop=((inner, width), bf16),
        lift=((width, inner), bf16),
        joint=((3, width, part), bf16),
        out=((part, width), bf16),
        dy=(full, bf16),
        wide_a=((packs, 2 * rows, inner), bf16),
        wide_b=((packs, 2 * rows, inner), bf16),
        narrow=(full, bf16),
        source=(full, bf16),
        dm_mine=(full, bf16),
        dm_peer=(full, bf16),
        dn_mine=(full, bf16),
        dn_peer=(full, bf16),
        crossed=(full, bf16),
        middle=(full, f32),
        dmid=(full, f32),
        da=(full, bf16),
        inv=((2 * rows, part), f32),
        ends=((packs, rows, width), f32),
        ends_mine=((packs, rows, width), bf16),
        ends_peer=((packs, rows, width), bf16),
        e=((2, 2, 2 * rows, 2 * rows), bf16),
        dc=((2 * rows, part), f32),
        dprob=((2, 2 * rows, 2 * rows), f32),
        ds=((2, 2 * rows, 2 * rows), bf16),
        staged=((2, 2, 4, block // 8, width), bf16),
        sums=((2, 8, width), f32),
        sums_peer=((2, 8, width), f32),
        tail=((4, block // 8, width), bf16),
    )
    sem = pltpu.SemaphoreType.DMA
    flags = dict(
        load=sem((LOADS,)),
        e_load=sem((2,)),
        x_send=sem((2, 2, packs)),
        x_recv=sem((2, 2, packs)),
        c_send=sem((packs,)),
        c_recv=sem((packs,)),
        g_store=sem((2,)),
        t_store=sem((2,)),
        v_send=sem((2,)),
        v_recv=sem((2,)),
        y_send=sem((packs,)),
        y_recv=sem((packs,)),
        o_keep=sem((1,)),
        o_send=sem((1,)),
        o_recv=sem((1,)),
    )
    return list(plan) + list(flags), [pltpu.VMEM(*spec) for spec in plan.values()] + list(flags.values())


def backward_kernel(line, count, packs, inside, names, *refs):
    refs = list(refs)

    def take(n):
        taken = refs[:n]
        del refs[:n]
        return taken

    small, dy_in, y_in = take(3)
    weights = [Names(zip(WEIGHTS, take(4))) for _ in range(2)]
    kept = [Names(zip(KEPT, take(len(KEPT)))) for _ in range(2)]
    edges_ref, *g_refs = take(3)
    o_ref = take(1)[0] if inside else None
    w = Names(zip(names, take(len(names))))
    core, half = lax.axis_index("section"), lax.axis_index("tensor")
    every, width = w.dy.shape[1:]
    rows = every // 2
    part, inner = w.out.shape[0], w.drop.shape[0]
    block = 8 * w.tail.shape[1]
    pairs = part // (2 * HEAD_DIM)
    x_peer = {"tensor": 1 - half}
    sibling = {"section": 1 - core}
    own = pl.multiple_of(half * rows, rows)
    theirs = pl.multiple_of((1 - half) * rows, rows)
    early = lax.broadcasted_iota(jnp.int32, (1, 2 * HEAD_DIM), 1) < HEAD_DIM
    numbers = iter(range(LOADS))
    down, across = ((0,), (0,)), ((1,), (1,))

    def fetch(src, dst):
        copy = pltpu.make_async_copy(src, dst, w.load.at[next(numbers)])
        copy.start()
        return copy

    def remote(src, dst, sent, got, target):
        return pltpu.make_async_remote_copy(
            src_ref=src, dst_ref=dst, send_sem=sent, recv_sem=got,
            device_id=target, device_id_type=MESH,
        )

    def over_x(src, dst, kind, s, m):
        return remote(src, dst, w.x_send.at[kind, s, m], w.x_recv.at[kind, s, m], x_peer)

    pending = {}

    def ask(key, src, dst):
        pending[key] = fetch(src, dst)

    def got(key):
        pending.pop(key).wait()

    def ask_layer(s):
        for name in ("drop", "lift"):
            ask(name, getattr(weights[s], name), getattr(w, name))

    def ask_rows(s):
        for m in range(packs):
            ask(("act", m), kept[s].act.at[m], w.wide_a.at[m])
            ask(("steep", m), kept[s].steep.at[m], w.wide_b.at[m])
            ask(("mixed", m), kept[s].mixed.at[m], w.narrow.at[m])

    def ask_attention(s):
        for name in ("joint", "out"):
            ask(name, getattr(weights[s], name), getattr(w, name))
        for m in range(packs):
            ask(("middle", m), kept[s].middle.at[m], w.middle.at[m])
        ask(("inv", 0), kept[s].inv.at[0], w.inv)

    for m in range(packs):
        ask(("dy", m), dy_in.at[m], w.dy.at[m])
        ask(("ends", m), y_in.at[m, pl.ds(own, rows)], w.ends_mine.at[m])
    ask_rows(1)
    ask_layer(1)
    ask_attention(1)

    clock, ready = [0], [0]
    if inside:
        greet, run_ticks, drain, length = reducer(
            line, count, g_refs, o_ref, refs[:BUFS], refs[BUFS:]
        )
        greet([x_peer])

        def ticks(n):
            n = min(n, ready[0] - clock[0])
            if n > 0:
                run_ticks(clock[0], clock[0] + n)
                clock[0] += n
    else:
        barrier = pltpu.get_barrier_semaphore()
        for target in (x_peer, sibling):
            pl.semaphore_signal(barrier, inc=1, device_id=target, device_id_type=MESH)
        pl.semaphore_wait(barrier, 2)

        def ticks(n):
            pass

    def add_sums(s, m, row, value):
        at = pl.ds(row, 1)
        w.sums[s, at] = value if m == 0 else w.sums[s, at] + value

    stores = [None, None]
    stored = [0]

    def emit(s, number, fill):
        slot = stored[0] % 2
        stored[0] += 1
        if stores[slot] is not None:
            stores[slot].wait()
        fill(slot)
        stores[slot] = pltpu.make_async_copy(
            w.staged.at[slot], g_refs[s].at[pl.ds(2 * number, 2)], w.g_store.at[slot]
        )
        stores[slot].start()

    def settle_stores():
        for slot in range(2):
            if stores[slot] is not None:
                stores[slot].wait()
                stores[slot] = None

    def put(slot, value, first=0, lanes=slice(None)):
        step = block // 8
        per = 4 * step
        for r in range(0, value.shape[0], step):
            at = first + r
            w.staged[slot, at // per, at % per // step, :, lanes] = low(value[r : r + step])

    def product(lefts, rights):
        return sum(dot(a[...], b[...], down) for a, b in zip(lefts, rights))

    dm = [[over_x(w.dm_mine.at[m], w.dm_peer.at[m], 0, s, m) for m in range(packs)] for s in range(2)]
    dn = [
        [
            over_x(
                w.dn_mine.at[m, pl.ds(theirs, rows)],
                w.dn_peer.at[m, pl.ds(0, rows)],
                1, 0, m,
            )
            for m in range(packs)
        ],
        [over_x(w.dn_mine.at[m], w.dn_peer.at[m], 1, 1, m) for m in range(packs)],
    ]

    def far_copy(m):
        return remote(w.dm_mine.at[m], w.crossed.at[m], w.c_send.at[m], w.c_recv.at[m], sibling)

    def feed_forward(s, m):
        got(("steep", m))
        if s == 0:
            pl.when(core == 1)(lambda: far_copy(m).wait_send())
        size = 256
        for number in range(inner // size):
            lanes = pl.ds(number * size, size)
            grad = dot(w.dy[m], w.drop[lanes], across) * wide(w.wide_b[m, :, lanes])
            grad = low(grad)
            w.wide_b[m, :, lanes] = grad
            total = column_sum(wide(grad))
            at = number * size
            spot = (s, pl.ds(VECTORS + at // width, 1), pl.ds(at % width, size))
            w.sums[spot] = total if m == 0 else w.sums[spot] + total
        add_sums(s, m, 5, 0.5 * column_sum(wide(w.dy[m])))
        for r in (0, rows):
            at = pl.ds(r, rows)
            w.dm_mine[m, at] = low(dot(w.wide_b[m, at], w.lift[...], across))
        dm[s][m].start()

    def drop_weights(s, spread):
        for m in range(packs):
            got(("act", m))
        for number, first in enumerate(range(0, inner, block)):
            lanes = pl.ds(first, block)
            value = product([w.wide_a.at[m, :, lanes] for m in range(packs)], [w.dy.at[m] for m in range(packs)])
            emit(s, number, lambda slot: put(slot, value))
            if number % 2:
                ticks(spread)
        settle_stores()
        ready[0] = (0 if s else count) + 2 * (inner // block)

    def lift_weights(s, spread):
        for m in range(packs):
            got(("mixed", m))
        number = inner // block
        for column in range(0, inner, width):
            for first in range(0, width, block):
                value = product(
                    [w.narrow.at[m, :, pl.ds(first, block)] for m in range(packs)],
                    [w.wide_b.at[m, :, pl.ds(column, width)] for m in range(packs)],
                )
                emit(s, number, lambda slot: put(slot, value))
                number += 1
                if number % 2 == 0:
                    ticks(spread)
        settle_stores()
        ready[0] = (0 if s else count) + 2 * number
        for m in range(packs):
            ask(("qkvc", m), kept[s].qkvc.at[m], w.wide_a.at[m])
            ask(("normed", m), kept[s].normed.at[m], w.narrow.at[m])
            if s:
                ask(("source", m), kept[s].source.at[m], w.source.at[m])
        ask_e(s, 0)

    def e_copy(s, number):
        m, pair = divmod(number, pairs)
        return pltpu.make_async_copy(
            kept[s].e.at[m, pl.ds(2 * pair, 2)], w.e.at[number % 2], w.e_load.at[number % 2]
        )

    def ask_e(s, number):
        if number < packs * pairs:
            e_copy(s, number).start()

    def attention(s, m, spread, between=None):
        if m == 0:
            got("out")
        got(("middle", m))
        if s:
            got(("ends", m))
            for r in range(0, rows, 32):
                at = pl.ds(r, 32)
                mine = w.middle[m, pl.ds(pl.multiple_of(own + r, 32), 32)]
                w.ends[m, at] = mine + wide(w.ends_mine[m, at]) + small[1, pl.ds(5, 1)]
        if m == 0:
            ticks(1)
        dm[s][m].wait()
        if s and m == packs - 1:
            for n in range(packs):
                ends_copy(n).start()
        totals = [0.0, 0.0, 0.0]
        for at in row_blocks(every, 32):
            grad = wide(w.dm_mine[m, at]) + wide(w.dm_peer[m, at])
            pulled, along = norm_rows_back(w.middle[m, at], grad, small[s, pl.ds(1, 1)])
            through = wide(w.dy[m, at]) + pulled
            w.dmid[m, at] = through
            da = low(through)
            w.da[m, at] = da
            for i, piece in enumerate((along, grad, wide(da))):
                totals[i] = totals[i] + column_sum(piece)
        for i, row in enumerate((1, 3, 4)):
            add_sums(s, m, row, 0.5 * totals[i])
        ticks(1)
        got(("inv", m))
        w.dc[...] = dot(w.da[m], w.out[...], across) * w.inv[...]
        if m + 1 < packs:
            ask(("inv", m + 1), kept[s].inv.at[m + 1], w.inv)
        got(("qkvc", m))
        for pair in range(pairs):
            number = m * pairs + pair
            e_copy(s, number).wait()
            ask_e(s, number + 1)
            e_ref = w.e.at[number % 2]

            def lanes(i):
                return pl.ds(i * part + pair * 2 * HEAD_DIM, 2 * HEAD_DIM)

            queries, keys, values = (w.wide_a[m, :, lanes(i)] for i in range(3))
            grad = low(w.dc[:, lanes(0)])
            for side in range(2):
                here = early if side == 0 else jnp.logical_not(early)
                w.dprob[side] = dot(jnp.where(here, grad, 0), values, across)
            for side in range(2):
                here = early if side == 0 else jnp.logical_not(early)
                for at in row_blocks(every):
                    level = jnp.where(here, w.dc[at, lanes(0)] * wide(w.wide_a[m, at, lanes(3)]), 0.0)
                    level = jnp.sum(level, axis=-1, keepdims=True)
                    w.ds[side, at] = low(wide(e_ref[side, at]) * (w.dprob[side, at] - level))
            dv = [dot(e_ref[side], grad, down) for side in range(2)]
            w.wide_b[m, :, lanes(2)] = low(jnp.where(early, dv[0], dv[1]))
            dk = [dot(w.ds[side], queries, down) for side in range(2)]
            w.wide_b[m, :, lanes(1)] = low(jnp.where(early, dk[0], dk[1]))
            dq = [dot(w.ds[side], keys) for side in range(2)]
            w.wide_b[m, :, lanes(0)] = low(SCALE * jnp.where(early, dq[0], dq[1]))
            ticks(spread)
            if between is not None and pair == 0:
                between()
        if m == 0:
            got("joint")
        if s == 0:
            dn[1][m].wait_send()
        for r in (0, rows):
            at = pl.ds(r, rows)
            dq, dk, dv = (w.wide_b[m, at, pl.ds(i * part, part)] for i in range(3))
            far = dot(dk, w.joint[1], across) + dot(dv, w.joint[2], across)
            near = dot(dq, w.joint[0], across)
            if s:
                w.dm_mine[m, at] = low(far)
                w.middle[m, at] = near + jnp.where(core == 0, far, 0.0)
            else:
                w.dn_mine[m, at] = low(near + far)
        if s:
            pl.when(core == 1)(lambda: far_copy(m).start())
        else:
            dn[0][m].start()

    def join(m):
        pl.when(core == 0)(lambda: far_copy(m).wait_recv())
        for at in row_blocks(every, 32):
            there = jnp.where(core == 0, wide(w.crossed[m, at]), 0.0)
            w.dn_mine[m, at] = low(w.middle[m, at] + there)
        dn[1][m].start()

    def attention_weights(s, spread):
        for m in range(packs):
            got(("normed", m))
            if s:
                got(("source", m))
        normed = [w.narrow.at[m] for m in range(packs)]
        source = [w.source.at[m] for m in range(packs)] if s else normed
        dq, dk, dv = (
            [w.wide_b.at[m, :, pl.ds(i * part, part)] for m in range(packs)] for i in range(3)
        )
        context = [w.wide_a.at[m, :, pl.ds(3 * part, part)] for m in range(packs)]
        da = [w.da.at[m] for m in range(packs)]
        number = 2 * inner // block
        for first in range(0, width, block):
            at = pl.ds(first, block)
            query = product([n.at[:, at] for n in normed], dq)
            key = product([n.at[:, at] for n in source], dk)

            def both(slot):
                put(slot, query, 0, pl.ds(0, part))
                put(slot, key, 0, pl.ds(part, part))

            emit(s, number, both)
            number += 1
        ticks(spread)

        def values(slot):
            for side in range(width // part):
                at = pl.ds(side * part, part)
                put(slot, product([n.at[:, at] for n in source], dv), 0, at)

        emit(s, number, values)
        emit(s, number + 1, lambda slot: put(slot, product(context, da)))
        number += 2
        ticks(spread)
        settle_stores()
        ready[0] = (0 if s else count) + 2 * number

    def leave(s, m):
        dn[s][m].wait_recv()
        got(("base", m))
        totals = [0.0, 0.0]
        for r in range(0, every if s else rows, 32):
            peer, mine = pl.ds(r, 32), pl.ds(r if s else pl.multiple_of(own + r, 32), 32)
            grad = wide(w.dn_mine[m, mine]) + wide(w.dn_peer[m, peer])
            pulled, along = norm_rows_back(wide(w.source[m, peer]), grad, small[s, pl.ds(0, 1)])
            result = low(w.dmid[m, mine] + pulled)
            if s:
                w.dy[m, peer] = result
            else:
                w.ends_peer[m, peer] = result
            for i, piece in enumerate((along, grad)):
                totals[i] = totals[i] + column_sum(piece)
        scale = 0.5 if s else 1.0
        add_sums(s, m, 0, scale * totals[0])
        add_sums(s, m, 2, scale * totals[1])

    def vectors(s):
        return remote(w.sums.at[s], w.sums_peer.at[s], w.v_send.at[s], w.v_recv.at[s], x_peer)

    def tail_store(s):
        return pltpu.make_async_copy(w.tail, g_refs[s].at[count - 1], w.t_store.at[s])

    def finish_vectors(s):
        vectors(s).wait()
        row = lax.broadcasted_iota(jnp.int32, (8, 1), 0)
        total = w.sums[s] + jnp.where(row < VECTORS, w.sums_peer[s], 0.0)
        if s:
            w.tail[...] = jnp.zeros(w.tail.shape, w.tail.dtype)
        pad = jnp.zeros((w.tail.shape[1] - 8, width), jnp.float32)
        w.tail[0] = low(jnp.concatenate([total, pad]))
        tail_store(s).start()
        tail_store(s).wait()
        ready[0] = max(ready[0], count if s else 2 * count)

    def ends_copy(m):
        return remote(
            y_in.at[m, pl.ds(theirs, rows)], w.ends_peer.at[m], w.y_send.at[m], w.y_recv.at[m], x_peer
        )

    def ends(m):
        ends_copy(m).wait()
        for at in row_blocks(rows, 32):
            w.ends_mine[m, at] = low(w.ends[m, at] + wide(w.ends_peer[m, at]))

    def edges_keep(src, b):
        return pltpu.make_async_copy(src, edges_ref.at[b], w.o_keep.at[0])

    def edges_hand(src, b):
        return remote(src, edges_ref.at[b], w.o_send.at[0], w.o_recv.at[0], sibling)

    def ask_base(s):
        for m in range(packs):
            if s:
                ask(("base", m), kept[s].base.at[m], w.source.at[m])
            else:
                ask(("base", m), kept[s].base.at[m, pl.ds(own, rows)], w.source.at[m, pl.ds(0, rows)])

    for m in range(packs):
        got(("dy", m))
    drop_weights(1, 0)
    for s in (1, 0):
        for m in range(packs):
            if s == 0:
                ticks(1)
                leave(1, m)
            if m == 0:
                got("drop")
                got("lift")
            feed_forward(s, m)
            ticks(1)
        if s == 0:
            vectors(1).start()
            drop_weights(0, 1)
            finish_vectors(1)
            for m in range(packs):
                ends(m)
            pl.when(core == 0)(lambda: edges_hand(w.ends_mine, 0).start())
            pl.when(core == 1)(lambda: edges_keep(w.ends_mine, 1).start())
            ask_base(0)
        if s:
            ask_layer(0)
        lift_weights(s, 1)
        for m in range(packs):
            attention(s, m, 1, partial(join, m - 1) if s and m else None)
        if s:
            join(packs - 1)
            ask_attention(0)
        attention_weights(s, 1)
        if s:
            ask_base(1)
            ask_rows(0)
            ticks(1)
    for m in range(packs):
        leave(0, m)
        ticks(1)
    vectors(0).start()
    finish_vectors(0)
    pl.when(core == 0)(lambda: edges_keep(w.ends_peer, 0).start())
    pl.when(core == 1)(lambda: edges_hand(w.ends_peer, 1).start())
    if inside:
        run_ticks(clock[0], length)
        drain()
    for m in range(packs):
        dn[0][m].wait_send()
    edges_keep(w.ends_peer, 0).wait()
    edges_hand(w.ends_peer, 0).wait()


def backward(line, small, dy, ends, weights, kept, inside):
    packs, every, width = dy.shape
    rows = every // 2
    inner, part = weights[0][0].shape[0], weights[0][3].shape[0]
    block = 8 * CHUNK
    count = (2 * inner + 4 * part) // (4 * CHUNK) + 1
    chunks = shape((count, 4, CHUNK, width))
    args = [small, dy, ends] + [a for s in range(2) for a in weights[s]] + [a for s in range(2) for a in kept[s]]
    anywhere = pl.BlockSpec(memory_space=pl.ANY)
    outs = [shape((2, packs, rows, width)), chunks, chunks]
    if inside:
        outs.append(shape((2,) + chunks.shape))
    names, scratch = backward_scratch(packs, rows, width, part, inner, block)
    if inside:
        bufs, sems = reducer_scratch(line, CHUNK, width)
        scratch = scratch + bufs + sems
    return pl.pallas_call(
        partial(backward_kernel, line, count, packs, inside, names),
        out_shape=outs,
        in_specs=[pl.BlockSpec(memory_space=pltpu.VMEM)] + [anywhere] * (len(args) - 1),
        out_specs=[anywhere] * len(outs),
        scratch_shapes=scratch,
        compiler_params=pltpu.CompilerParams(
            collective_id=2, has_side_effects=True, vmem_limit_bytes=62 * 1024 * 1024
        ),
    )(*args)


def local(
    edges_in,
    joint_weight,
    output_weight,
    lift_weight,
    lift_bias,
    drop_weight,
    norm_gains,
    norm_shifts,
    branch_biases,
    item_lengths,
    key_keep,
):
    half = lax.axis_index("tensor")
    held = edges_in[0]
    packs, _, width = held.shape[1:]
    part = joint_weight.shape[-1]
    inner = lift_weight.shape[-1]
    heads = part // HEAD_DIM
    head_ids = wide(half * heads + jnp.arange(heads, dtype=jnp.int32))
    slopes = jnp.power(2.0, -8.0 * (head_ids + 1.0) / HEADS)

    small = jnp.concatenate(
        [norm_gains[0], norm_shifts[0], branch_biases[0], lift_bias[0].reshape(2, -1, width)], axis=1
    )
    small = jnp.concatenate([small, jnp.zeros((2, 16 - small.shape[1], width), small.dtype)], axis=1)
    distances = [masked_distance(item_lengths[0, m], key_keep[0, m]) for m in range(packs)]
    given = (joint_weight[0], output_weight[0], small, lift_weight[0], drop_weight[0])
    kept, weights, small, dy, ends = forward(slopes, held, distances, given)
    line = lax.axis_size("dp") // 2
    inside = line == 4
    edges_out, *grads = backward(line, small, dy, ends, weights, kept, inside)
    grads = grads[2] if inside else reduce_over_dp(grads, line)
    grads = grads.reshape(2, -1, width)
    drop_grad, lift_grad, joint_grad, output_grad, *vectors, lift_total = widened(grads, inner, part)
    return (
        edges_out[None],
        joint_grad[None],
        output_grad[None],
        lift_grad[None],
        lift_total[None],
        drop_grad[None],
        vectors[0][None],
        vectors[1][None],
        vectors[2][None],
    )


def solution(mesh):
    in_specs = (
        P("section", None, None, ("dp", "tensor"), None),
        P("section", None, None, None, "tensor"),
        P("section", None, "tensor", None),
        P("section", None, None, "tensor"),
        P("section", None, "tensor"),
        P("section", None, "tensor", None),
        P("section", None, None, None),
        P("section", None, None, None),
        P("section", None, None, None),
        P("dp", None, None),
        P("dp", None, None),
    )
    out_specs = (
        P("section", None, None, ("dp", "tensor"), None),
        P("section", None, None, None, "tensor"),
        P("section", None, "tensor", None),
        P("section", None, None, "tensor"),
        P("section", None, "tensor"),
        P("section", None, "tensor", None),
        P("section", None, None, None),
        P("section", None, None, None),
        P("section", None, None, None),
    )
    return jax.shard_map(local, mesh=mesh, in_specs=in_specs, out_specs=out_specs, check_vma=False)
```
